256 devices in a mesh: fsdp: 16 (over z, core), grp: 16 (over y, x).
Axes of the slice: x: 4, y: 4, z: 8, core: 2. Of those that a mesh axis runs over, the one named last changes fastest.
Arguments:
- grads: bfloat16 [16, 1536, 4096], P(None, 'fsdp', 'grp')
- owner: int32 [16], replicated, may hold values from 0 to 15, as said below
Outputs:
- update: bfloat16 [16, 1536, 4096], P(None, 'fsdp', 'grp')
- owned: bfloat16 [32, 1536, 4096], P('fsdp', None, 'grp')
The draws below stay inside these ranges and needn't reach their ends.
Inputs may be any that keep to these rules, and one draw needn't show every extreme that they name: `owner`: no group owns more than 2 matrices, and some group owns exactly 2.
All inputs are finite; a program needn't handle non-finite values.
Results may differ from the reference program's by a relative error of at most 0.02.
Values may be sent and summed in bfloat16 or wider, within the bound.
No kernel may reach another device: no remote copies, remote signals or barrier semaphores. Data moves between devices by JAX's collectives and lax.ppermute only.
A program may use at most 64 MiB of HBM per device.

```python
import math
import jax
import jax.numpy as jnp
from jax import lax

ROWS = 1536
COLS = 4096
MOST = 2
MAT = 16
N_FSDP = 16
N_GRP = 16


def draw_grads(key, part):
    key = jax.random.fold_in(key, 11)
    first, second, third = jax.random.split(key, 3)
    base = jax.random.normal(first, (MAT, ROWS, COLS), jnp.float32)
    column_top = jnp.log(10.0)
    row_scale = jnp.exp(jax.random.uniform(second, (MAT, ROWS, 1), jnp.float32) * jnp.log(3.0))
    column_scale = jnp.exp(jax.random.uniform(third, (MAT, 1, COLS), jnp.float32) * column_top)
    return (base * row_scale * column_scale).astype(jnp.bfloat16)


def draw_owner(key, part):
    key = jax.random.fold_in(key, 7)
    first, second = jax.random.split(key)
    groups = jax.random.permutation(first, MAT).astype(jnp.int32)
    quarter = MAT // 4
    listed = jnp.concatenate([groups[:quarter], groups[:quarter], groups[quarter:3 * quarter]])
    order = jax.random.permutation(second, MAT)
    return listed[order].astype(jnp.int32)


def setup_inputs(seed: int = 0) -> dict:
    seeds = jax.random.split(jax.random.key(seed), 3)
    grads = draw_grads(jax.random.fold_in(seeds[2], 71), 0)
    owner = draw_owner(jax.random.fold_in(seeds[2], 71), 0)
    return dict(grads=grads, owner=owner)


def orthogonal(grad):
    values = grad.astype(jnp.float32)
    total = jnp.sum(values * values) / ROWS
    normed = (values * (1.0 / jnp.sqrt(total + 1e-06))).astype(jnp.bfloat16)
    blocks = normed.reshape(ROWS, N_GRP, COLS // N_GRP).astype(jnp.float32)
    terms = jnp.einsum('rkc,skc->krs', blocks, blocks).astype(jnp.bfloat16)
    terms = lax.optimization_barrier(terms)
    gram = lax.optimization_barrier(jnp.sum(terms.astype(jnp.float32), axis=0)).astype(jnp.bfloat16)
    left = jnp.dot(gram, normed, preferred_element_type=jnp.float32).astype(jnp.bfloat16)
    right = jnp.dot(gram, left, preferred_element_type=jnp.float32)
    factor = 0.2 * math.sqrt(max(ROWS, COLS))
    mixed = 3.4445 * normed.astype(jnp.float32) - 4.775 * left.astype(jnp.float32) + 2.0315 * right
    return (factor * mixed).astype(jnp.bfloat16)

def reference(grads, owner):
    update = lax.map(orthogonal, grads)
    index = jnp.arange(MAT, dtype=jnp.int32)
    same = (owner[:, None] == owner[None, :]) & (index[None, :] < index[:, None])
    rank = lax.optimization_barrier(jnp.sum(same.astype(jnp.int32), axis=1)).astype(jnp.int32)
    target = (owner * MOST + rank).astype(jnp.int32)
    owned = jnp.zeros((N_FSDP * MOST, ROWS, COLS), jnp.bfloat16).at[target].set(update)
    return (update, owned)
```

```python
import functools
import math

import jax
import jax.numpy as jnp
from jax import lax
from jax.experimental import pallas as pl
from jax.experimental.pallas import tpu as pltpu
from jax.sharding import PartitionSpec as P

MOST = 2
SIDE = 4
BLOCK = 256
HALF = 128
PIECE = BLOCK // SIDE
SUB = PIECE // SIDE
VMEM_LIMIT = 56 * 1024 * 1024

VMEM = pl.BlockSpec(memory_space=pltpu.VMEM)
SMEM = pl.BlockSpec(memory_space=pltpu.SMEM)


def params():
    return pltpu.CompilerParams(vmem_limit_bytes=VMEM_LIMIT)


def shape_of(*dims, dtype=jnp.bfloat16):
    return jax.ShapeDtypeStruct(dims, dtype)


def pairs_of(rows):
    side = rows // BLOCK
    return [(i, j) for i in range(side) for j in range(i + 1)]


def plan_kernel(owner_ref, grads_ref, table_ref, packed_ref, empty_ref):
    count = owner_ref.shape[0]

    def clear(g, _):
        table_ref[2, g] = -1
        table_ref[3, g] = 0
        return 0

    lax.fori_loop(0, count, clear, 0)

    def first(e, _):
        g = owner_ref[e]
        seen = table_ref[3, g]
        table_ref[3, g] = seen + 1

        @pl.when(seen == 0)
        def _():
            table_ref[0, g] = e
            table_ref[1, e] = g

        @pl.when(seen > 0)
        def _():
            table_ref[2, g] = e

        return 0

    lax.fori_loop(0, count, first, 0)

    def empties(g, n):
        none = table_ref[3, g] == 0

        @pl.when(none)
        def _():
            empty_ref[n] = g

        return n + none.astype(jnp.int32)

    lax.fori_loop(0, count, empties, 0)

    def second(g, n):
        e = table_ref[2, g]
        two = e >= 0

        @pl.when(two)
        def _():
            h = empty_ref[n]
            table_ref[2, g] = h
            table_ref[0, h] = e
            table_ref[1, e] = h

        return n + two.astype(jnp.int32)

    lax.fori_loop(0, count, second, 0)

    def move(g, _):
        packed_ref[g] = grads_ref[table_ref[0, g]]
        return 0

    lax.fori_loop(0, count, move, 0)


def plan(owner, grads):
    count = grads.shape[0]
    return pl.pallas_call(
        plan_kernel,
        out_shape=(shape_of(4, count, dtype=jnp.int32), shape_of(*grads.shape)),
        in_specs=[SMEM, VMEM],
        out_specs=(SMEM, VMEM),
        scratch_shapes=[pltpu.SMEM((count,), jnp.int32)],
        compiler_params=params(),
        name="plan",
    )(owner, grads)


def gram_kernel(pairs, place_ref, x_ref, *refs):
    outs, square_ref, full = refs[: 2 * SIDE], refs[2 * SIDE], refs[2 * SIDE + 1]
    for t, (i, j) in enumerate(pairs):
        full[t] = lax.dot_general(
            x_ref[i * BLOCK : (i + 1) * BLOCK, :],
            x_ref[j * BLOCK : (j + 1) * BLOCK, :],
            (((1,), (1,)), ((), ())),
            preferred_element_type=jnp.float32,
        ).astype(jnp.bfloat16)
        for half in range(2):
            for s in range(SIDE):
                p = lax.rem(place_ref[half] + s, SIDE)
                rows = pl.ds(pl.multiple_of(p * PIECE, PIECE), PIECE)
                outs[half * SIDE + s][t] = full[t, rows, half * HALF : (half + 1) * HALF]
    total = jnp.zeros((1, x_ref.shape[1]), jnp.float32)
    for i in range(x_ref.shape[0] // BLOCK):
        values = x_ref[i * BLOCK : (i + 1) * BLOCK, :].astype(jnp.float32)
        total = total + jnp.sum(values * values, axis=0, keepdims=True)
    total = jnp.sum(total, axis=1, keepdims=True)
    square_ref[...] = jnp.broadcast_to(total, square_ref.shape)


def gram_terms(place, x):
    pairs = pairs_of(x.shape[0])
    piece = shape_of(len(pairs), PIECE, HALF)
    return pl.pallas_call(
        functools.partial(gram_kernel, pairs),
        out_shape=(piece,) * (2 * SIDE) + (shape_of(8, HALF, dtype=jnp.float32),),
        in_specs=[SMEM, VMEM],
        out_specs=(VMEM,) * (2 * SIDE + 1),
        scratch_shapes=[pltpu.VMEM((len(pairs), BLOCK, BLOCK), jnp.bfloat16)],
        compiler_params=params(),
        name="gram",
    )(place, x)


def add_kernel(place_ref, *refs):
    ins, outs = refs[: 2 * SIDE], refs[2 * SIDE : 4 * SIDE]
    for half in range(2):
        got = ins[half * SIDE : (half + 1) * SIDE]
        for s in range(SIDE):
            p = lax.rem(place_ref[1 - half] + s, SIDE)
            rows = pl.ds(pl.multiple_of(p * SUB, SUB), SUB)
            total = got[0][:, rows, :].astype(jnp.float32)
            for other in got[1:]:
                total = total + other[:, rows, :].astype(jnp.float32)
            outs[half * SIDE + s][...] = total.astype(jnp.bfloat16)


def add_first(place, pieces):
    blocks = pieces[0].shape[0]
    return pl.pallas_call(
        add_kernel,
        out_shape=(shape_of(blocks, SUB, HALF),) * (2 * SIDE),
        in_specs=[SMEM] + [VMEM] * (2 * SIDE),
        out_specs=(VMEM,) * (2 * SIDE),
        compiler_params=params(),
        name="add_first",
    )(place, *pieces)


def add_last_kernel(square_ref, *refs):
    ins, outs = refs[: 2 * SIDE], refs[2 * SIDE :]
    blocks = ins[0].shape[0]
    for half in range(2):
        got = ins[half * SIDE : (half + 1) * SIDE]
        total = got[0][...].astype(jnp.float32)
        for other in got[1:]:
            total = total + other[...].astype(jnp.float32)
        outs[half][:blocks] = total.astype(jnp.bfloat16)
    rest = jnp.broadcast_to(square_ref[0:1, :], (SUB, HALF))
    row = lax.broadcasted_iota(jnp.int32, (SUB, HALF), 0)
    parts = jnp.zeros((SUB, HALF), jnp.float32)
    for k in range(3):
        top = lax.reduce_precision(rest, 8, 7)
        parts = jnp.where(row == k, top, parts)
        rest = rest - top
    outs[0][blocks] = parts.astype(jnp.bfloat16)


def add_last(square, pieces):
    blocks = pieces[0].shape[0]
    return pl.pallas_call(
        add_last_kernel,
        out_shape=(shape_of(blocks + 1, SUB, HALF), shape_of(blocks, SUB, HALF)),
        in_specs=[VMEM] * (2 * SIDE + 1),
        out_specs=(VMEM,) * 2,
        compiler_params=params(),
        name="add_last",
    )(square, *pieces)


def join_kernel(place_ref, *refs):
    ins, outs = refs[: 2 * SIDE], refs[2 * SIDE :]
    for half in range(2):
        for s in range(SIDE):
            p = lax.rem(place_ref[1 - half] - s + SIDE, SIDE)
            rows = pl.ds(pl.multiple_of(p * SUB, SUB), SUB)
            outs[half][:, rows, :] = ins[half * SIDE + s][...]


def join(place, parts):
    return pl.pallas_call(
        join_kernel,
        out_shape=tuple(
            shape_of(parts[half * SIDE].shape[0], PIECE, HALF) for half in range(2)
        ),
        in_specs=[SMEM] + [VMEM] * (2 * SIDE),
        out_specs=(VMEM,) * 2,
        compiler_params=params(),
        name="join",
    )(place, *parts)


def step_kernel(pairs, rows_all, factor, place_ref, x_ref, *refs):
    ins = refs[: 2 * SIDE]
    out_ref, gram, normed, left = refs[2 * SIDE :]
    blocks = len(pairs)
    total = jnp.zeros((1, HALF), jnp.float32)
    for s in range(SIDE):
        total = total + jnp.sum(ins[s][blocks].astype(jnp.float32), axis=0, keepdims=True)
    inverse = 1.0 / jnp.sqrt(total / rows_all + 1e-06)
    scale = inverse * inverse
    side = rows_all // BLOCK
    for i in range(side):
        rows = slice(i * BLOCK, (i + 1) * BLOCK)
        for half in range(2):
            lanes = slice(half * HALF, (half + 1) * HALF)
            normed[rows, lanes] = (x_ref[rows, lanes].astype(jnp.float32) * inverse).astype(
                jnp.bfloat16
            )
    for t, (i, j) in enumerate(pairs):
        for half in range(2):
            start = j * BLOCK + half * HALF
            for s in range(SIDE):
                p = lax.rem(place_ref[half] - s + SIDE, SIDE)
                rows = pl.ds(pl.multiple_of(i * BLOCK + p * PIECE, PIECE), PIECE)
                values = ins[half * SIDE + s][t].astype(jnp.float32) * scale
                gram[rows, start : start + HALF] = jnp.where(scale > 0, values, 0.0).astype(
                    jnp.bfloat16
                )
    for i, j in pairs:
        if i != j:
            block = gram[i * BLOCK : (i + 1) * BLOCK, j * BLOCK : (j + 1) * BLOCK]
            gram[j * BLOCK : (j + 1) * BLOCK, i * BLOCK : (i + 1) * BLOCK] = block.T
    for i in range(side):
        rows = slice(i * BLOCK, (i + 1) * BLOCK)
        left[rows, :] = jnp.dot(
            gram[rows, :], normed[...], preferred_element_type=jnp.float32
        ).astype(jnp.bfloat16)
    for i in range(side):
        rows = slice(i * BLOCK, (i + 1) * BLOCK)
        right = jnp.dot(gram[rows, :], left[...], preferred_element_type=jnp.float32)
        mixed = (
            3.4445 * normed[rows, :].astype(jnp.float32)
            - 4.775 * left[rows, :].astype(jnp.float32)
            + 2.0315 * right
        )
        out_ref[rows, :] = (factor * mixed).astype(jnp.bfloat16)


def step(place, x, pieces, factor):
    rows, cols = x.shape
    pairs = pairs_of(rows)
    return pl.pallas_call(
        functools.partial(step_kernel, pairs, rows, factor),
        out_shape=shape_of(rows, cols),
        in_specs=[SMEM, VMEM] + [VMEM] * (2 * SIDE),
        out_specs=VMEM,
        scratch_shapes=[
            pltpu.VMEM((rows, rows), jnp.bfloat16),
            pltpu.VMEM((rows, cols), jnp.bfloat16),
            pltpu.VMEM((rows, cols), jnp.bfloat16),
        ],
        compiler_params=params(),
        name="step",
    )(place, x, *pieces)


def deal_kernel(table_ref, back_ref, update_ref, second_ref):
    count = back_ref.shape[0]

    def move(e, _):
        update_ref[e] = back_ref[table_ref[1, e]]
        helper = table_ref[2, e]
        block = back_ref[jnp.maximum(helper, 0)]
        second_ref[e] = jnp.where(helper >= 0, block, jnp.zeros_like(block))
        return 0

    lax.fori_loop(0, count, move, 0)


def deal(table, back):
    return pl.pallas_call(
        deal_kernel,
        out_shape=(shape_of(*back.shape),) * 2,
        in_specs=[SMEM, VMEM],
        out_specs=(VMEM,) * 2,
        compiler_params=params(),
        name="deal",
    )(table, back)


def shift(value, axis, amount):
    moves = []
    for at in range(SIDE * SIDE):
        y, x = divmod(at, SIDE)
        if axis == 0:
            x = (x + amount) % SIDE
        else:
            y = (y + amount) % SIDE
        moves.append((at, y * SIDE + x))
    return lax.ppermute(value, "grp", moves)


def spread(send, axes):
    got = {(half, 0): send[half][0] for half in range(2)}
    for s in (1, 3, 2):
        for half in range(2):
            got[half, s] = shift(send[half][s], axes[half], s)
    return [got[half, s] for half in range(2) for s in range(SIDE)]


def on_device(grads, owner):
    count, rows_dev, cols_dev = grads.shape
    groups = lax.axis_size("fsdp")
    rows = rows_dev * groups
    cols = cols_dev * lax.axis_size("grp")
    factor = 0.2 * math.sqrt(max(rows, cols))
    at = lax.axis_index("grp")
    me = lax.axis_index("fsdp")
    place = jnp.stack([lax.rem(at, SIDE), lax.div(at, SIDE)]).astype(jnp.int32)
    table, packed = plan(owner, grads)
    x = lax.all_to_all(packed, "fsdp", split_axis=0, concat_axis=0, tiled=True)
    x = x.reshape(rows, cols_dev)
    *terms, square = gram_terms(place, x)
    pieces = spread((terms[:SIDE], terms[SIDE:]), (0, 1))
    parts = add_first(place, pieces)
    parts = spread((parts[:SIDE], parts[SIDE:]), (1, 0))
    own = add_last(square, parts)
    parts = spread(([own[0]] * SIDE, [own[1]] * SIDE), (1, 0))
    own = join(place, parts)
    pieces = spread(([own[0]] * SIDE, [own[1]] * SIDE), (0, 1))
    done = step(place, x, pieces, factor)
    back = lax.all_to_all(
        done.reshape(count, rows_dev, cols_dev), "fsdp", split_axis=0, concat_axis=0, tiled=True
    )
    update, second = deal(table, back)
    second = lax.all_to_all(second, "fsdp", split_axis=0, concat_axis=0, tiled=True)
    first = jnp.where(table[3, me] > 0, done, jnp.zeros_like(done))
    owned = jnp.stack([first, second.reshape(rows, cols_dev)], axis=0)
    return (update, owned)


def solution(mesh):
    return jax.shard_map(
        on_device,
        mesh=mesh,
        in_specs=(P(None, "fsdp", "grp"), P()),
        out_specs=(P(None, "fsdp", "grp"), P("fsdp", None, "grp")),
        check_vma=False,
    )
```

```python
import functools
import math

import jax
import jax.numpy as jnp
from jax import lax
from jax.experimental import pallas as pl
from jax.experimental.pallas import tpu as pltpu
from jax.sharding import PartitionSpec as P

MOST = 2
SIDE = 4
BLOCK = 256
PIECE = BLOCK // SIDE
SUB = PIECE // SIDE
VMEM_LIMIT = 56 * 1024 * 1024

VMEM = pl.BlockSpec(memory_space=pltpu.VMEM)
SMEM = pl.BlockSpec(memory_space=pltpu.SMEM)


def params():
    return pltpu.CompilerParams(vmem_limit_bytes=VMEM_LIMIT)


def shape_of(*dims, dtype=jnp.bfloat16):
    return jax.ShapeDtypeStruct(dims, dtype)


def part(at, size):
    return pl.ds(pl.multiple_of(lax.rem(at, SIDE) * size, size), size)


def pairs_of(rows):
    side = rows // BLOCK
    return [(i, j) for i in range(side) for j in range(i + 1)]


def plan_kernel(owner_ref, grads_ref, table_ref, packed_ref, empty_ref):
    count = owner_ref.shape[0]

    def clear(g, _):
        table_ref[2, g] = -1
        table_ref[3, g] = 0
        return 0

    lax.fori_loop(0, count, clear, 0)

    def first(e, _):
        g = owner_ref[e]
        seen = table_ref[3, g]
        table_ref[3, g] = seen + 1

        @pl.when(seen == 0)
        def _():
            table_ref[0, g] = e
            table_ref[1, e] = g

        @pl.when(seen > 0)
        def _():
            table_ref[2, g] = e

        return 0

    lax.fori_loop(0, count, first, 0)

    def empties(g, n):
        none = table_ref[3, g] == 0

        @pl.when(none)
        def _():
            empty_ref[n] = g

        return n + none.astype(jnp.int32)

    lax.fori_loop(0, count, empties, 0)

    def second(g, n):
        e = table_ref[2, g]
        two = e >= 0

        @pl.when(two)
        def _():
            h = empty_ref[n]
            table_ref[2, g] = h
            table_ref[0, h] = e
            table_ref[1, e] = h

        return n + two.astype(jnp.int32)

    lax.fori_loop(0, count, second, 0)

    def move(g, _):
        packed_ref[g] = grads_ref[table_ref[0, g]]
        return 0

    lax.fori_loop(0, count, move, 0)


def plan(owner, grads):
    count = grads.shape[0]
    return pl.pallas_call(
        plan_kernel,
        out_shape=(shape_of(4, count, dtype=jnp.int32), shape_of(*grads.shape)),
        in_specs=[SMEM, VMEM],
        out_specs=(SMEM, VMEM),
        scratch_shapes=[pltpu.SMEM((count,), jnp.int32)],
        compiler_params=params(),
        name="plan",
    )(owner, grads)


def gram_kernel(pairs, place_ref, x_ref, *refs):
    outs, square_ref, full = refs[:SIDE], refs[SIDE], refs[SIDE + 1]
    for t, (i, j) in enumerate(pairs):
        full[t] = lax.dot_general(
            x_ref[i * BLOCK : (i + 1) * BLOCK, :],
            x_ref[j * BLOCK : (j + 1) * BLOCK, :],
            (((1,), (1,)), ((), ())),
            preferred_element_type=jnp.float32,
        ).astype(jnp.bfloat16)
        for s in range(SIDE):
            outs[s][t] = full[t, part(place_ref[0] + s, PIECE), :]
    total = jnp.zeros((1, x_ref.shape[1]), jnp.float32)
    for i in range(x_ref.shape[0] // BLOCK):
        values = x_ref[i * BLOCK : (i + 1) * BLOCK, :].astype(jnp.float32)
        total = total + jnp.sum(values * values, axis=0, keepdims=True)
    total = jnp.sum(total, axis=1, keepdims=True)
    square_ref[...] = jnp.broadcast_to(total, square_ref.shape)


def gram_terms(place, x):
    pairs = pairs_of(x.shape[0])
    return pl.pallas_call(
        functools.partial(gram_kernel, pairs),
        out_shape=(shape_of(len(pairs), PIECE, BLOCK),) * SIDE
        + (shape_of(8, BLOCK, dtype=jnp.float32),),
        in_specs=[SMEM, VMEM],
        out_specs=(VMEM,) * (SIDE + 1),
        scratch_shapes=[pltpu.VMEM((len(pairs), BLOCK, BLOCK), jnp.bfloat16)],
        compiler_params=params(),
        name="gram",
    )(place, x)


def add_kernel(place_ref, *refs):
    ins, outs = refs[:SIDE], refs[SIDE:]
    for s in range(SIDE):
        rows = part(place_ref[1] + s, SUB)
        total = ins[0][:, rows, :].astype(jnp.float32)
        for other in ins[1:]:
            total = total + other[:, rows, :].astype(jnp.float32)
        outs[s][...] = total.astype(jnp.bfloat16)


def add_first(place, pieces):
    blocks = pieces[0].shape[0]
    return pl.pallas_call(
        add_kernel,
        out_shape=(shape_of(blocks, SUB, BLOCK),) * SIDE,
        in_specs=[SMEM] + [VMEM] * SIDE,
        out_specs=(VMEM,) * SIDE,
        compiler_params=params(),
        name="add_first",
    )(place, *pieces)


def add_last_kernel(square_ref, *refs):
    ins, out = refs[:SIDE], refs[SIDE]
    blocks = ins[0].shape[0]
    total = ins[0][...].astype(jnp.float32)
    for other in ins[1:]:
        total = total + other[...].astype(jnp.float32)
    out[:blocks] = total.astype(jnp.bfloat16)
    rest = jnp.broadcast_to(square_ref[0:1, :], (SUB, BLOCK))
    row = lax.broadcasted_iota(jnp.int32, (SUB, BLOCK), 0)
    parts = jnp.zeros((SUB, BLOCK), jnp.float32)
    for k in range(3):
        top = lax.reduce_precision(rest, 8, 7)
        parts = jnp.where(row == k, top, parts)
        rest = rest - top
    out[blocks] = parts.astype(jnp.bfloat16)


def add_last(square, pieces):
    blocks = pieces[0].shape[0]
    return pl.pallas_call(
        add_last_kernel,
        out_shape=shape_of(blocks + 1, SUB, BLOCK),
        in_specs=[VMEM] * (SIDE + 1),
        out_specs=VMEM,
        compiler_params=params(),
        name="add_last",
    )(square, *pieces)


def join_kernel(place_ref, *refs):
    ins, out = refs[:SIDE], refs[SIDE]
    for s in range(SIDE):
        out[:, part(place_ref[1] - s + SIDE, SUB), :] = ins[s][...]


def join(place, parts):
    return pl.pallas_call(
        join_kernel,
        out_shape=shape_of(parts[0].shape[0], PIECE, BLOCK),
        in_specs=[SMEM] + [VMEM] * SIDE,
        out_specs=VMEM,
        compiler_params=params(),
        name="join",
    )(place, *parts)


def step_kernel(pairs, rows_all, factor, place_ref, x_ref, *refs):
    ins = refs[:SIDE]
    out_ref, gram, normed, left = refs[SIDE:]
    blocks = len(pairs)
    total = jnp.zeros((1, BLOCK), jnp.float32)
    for s in range(SIDE):
        total = total + jnp.sum(ins[s][blocks].astype(jnp.float32), axis=0, keepdims=True)
    inverse = 1.0 / jnp.sqrt(total / rows_all + 1e-06)
    scale = inverse * inverse
    side = rows_all // BLOCK
    for i in range(side):
        rows = slice(i * BLOCK, (i + 1) * BLOCK)
        normed[rows, :] = (x_ref[rows, :].astype(jnp.float32) * inverse).astype(jnp.bfloat16)
    for t, (i, j) in enumerate(pairs):
        for s in range(SIDE):
            p = lax.rem(place_ref[0] - s + SIDE, SIDE)
            rows = pl.ds(pl.multiple_of(i * BLOCK + p * PIECE, PIECE), PIECE)
            values = ins[s][t].astype(jnp.float32) * scale
            gram[rows, j * BLOCK : (j + 1) * BLOCK] = jnp.where(scale > 0, values, 0.0).astype(
                jnp.bfloat16
            )
    for i, j in pairs:
        if i != j:
            block = gram[i * BLOCK : (i + 1) * BLOCK, j * BLOCK : (j + 1) * BLOCK]
            gram[j * BLOCK : (j + 1) * BLOCK, i * BLOCK : (i + 1) * BLOCK] = block.T
    for i in range(side):
        rows = slice(i * BLOCK, (i + 1) * BLOCK)
        left[rows, :] = jnp.dot(
            gram[rows, :], normed[...], preferred_element_type=jnp.float32
        ).astype(jnp.bfloat16)
    for i in range(side):
        rows = slice(i * BLOCK, (i + 1) * BLOCK)
        right = jnp.dot(gram[rows, :], left[...], preferred_element_type=jnp.float32)
        mixed = (
            3.4445 * normed[rows, :].astype(jnp.float32)
            - 4.775 * left[rows, :].astype(jnp.float32)
            + 2.0315 * right
        )
        out_ref[rows, :] = (factor * mixed).astype(jnp.bfloat16)


def step(place, x, pieces, factor):
    rows, cols = x.shape
    pairs = pairs_of(rows)
    return pl.pallas_call(
        functools.partial(step_kernel, pairs, rows, factor),
        out_shape=shape_of(rows, cols),
        in_specs=[SMEM, VMEM] + [VMEM] * SIDE,
        out_specs=VMEM,
        scratch_shapes=[
            pltpu.VMEM((rows, rows), jnp.bfloat16),
            pltpu.VMEM((rows, cols), jnp.bfloat16),
            pltpu.VMEM((rows, cols), jnp.bfloat16),
        ],
        compiler_params=params(),
        name="step",
    )(place, x, *pieces)


def deal_kernel(table_ref, back_ref, update_ref, second_ref):
    count = back_ref.shape[0]

    def move(e, _):
        update_ref[e] = back_ref[table_ref[1, e]]
        helper = table_ref[2, e]
        block = back_ref[jnp.maximum(helper, 0)]
        second_ref[e] = jnp.where(helper >= 0, block, jnp.zeros_like(block))
        return 0

    lax.fori_loop(0, count, move, 0)


def deal(table, back):
    return pl.pallas_call(
        deal_kernel,
        out_shape=(shape_of(*back.shape),) * 2,
        in_specs=[SMEM, VMEM],
        out_specs=(VMEM,) * 2,
        compiler_params=params(),
        name="deal",
    )(table, back)


def spread(send, order):
    groups, places = lax.axis_size("fsdp"), SIDE * SIDE
    got = [send[0]]
    for amount in range(1, SIDE):
        moves = []
        for at in range(groups * places):
            group, place = divmod(at, places)
            y, x = divmod(place, SIDE)
            if group % 2 == order:
                x = (x + amount) % SIDE
            else:
                y = (y + amount) % SIDE
            moves.append((at, group * places + y * SIDE + x))
        got.append(lax.ppermute(send[amount], ("fsdp", "grp"), moves))
    return got


def on_device(grads, owner):
    count, rows_dev, cols_dev = grads.shape
    groups = lax.axis_size("fsdp")
    rows = rows_dev * groups
    cols = cols_dev * lax.axis_size("grp")
    factor = 0.2 * math.sqrt(max(rows, cols))
    at = lax.axis_index("grp")
    me = lax.axis_index("fsdp")
    along = jnp.stack([lax.rem(at, SIDE), lax.div(at, SIDE)]).astype(jnp.int32)
    place = jnp.where(lax.rem(me, 2) == 0, along, along[::-1])
    table, packed = plan(owner, grads)
    x = lax.all_to_all(packed, "fsdp", split_axis=0, concat_axis=0, tiled=True)
    x = x.reshape(rows, cols_dev)
    *terms, square = gram_terms(place, x)
    parts = add_first(place, spread(terms, 0))
    own = add_last(square, spread(parts, 1))
    own = join(place, spread([own] * SIDE, 1))
    done = step(place, x, spread([own] * SIDE, 0), factor)
    back = lax.all_to_all(
        done.reshape(count, rows_dev, cols_dev), "fsdp", split_axis=0, concat_axis=0, tiled=True
    )
    update, second = deal(table, back)
    second = lax.all_to_all(second, "fsdp", split_axis=0, concat_axis=0, tiled=True)
    first = jnp.where(table[3, me] > 0, done, jnp.zeros_like(done))
    owned = jnp.stack([first, second.reshape(rows, cols_dev)], axis=0)
    return (update, owned)


def solution(mesh):
    return jax.shard_map(
        on_device,
        mesh=mesh,
        in_specs=(P(None, "fsdp", "grp"), P()),
        out_specs=(P(None, "fsdp", "grp"), P("fsdp", None, "grp")),
        check_vma=False,
    )
```

```python
import functools
import math

import jax
import jax.numpy as jnp
from jax import lax
from jax.experimental import pallas as pl
from jax.experimental.pallas import tpu as pltpu
from jax.sharding import PartitionSpec as P

MOST = 2
SIDE = 4
BLOCK = 256
PIECE = BLOCK // SIDE
VMEM_LIMIT = 56 * 1024 * 1024

VMEM = pl.BlockSpec(memory_space=pltpu.VMEM)
SMEM = pl.BlockSpec(memory_space=pltpu.SMEM)


def params():
    return pltpu.CompilerParams(vmem_limit_bytes=VMEM_LIMIT)


def shape_of(*dims, dtype=jnp.bfloat16):
    return jax.ShapeDtypeStruct(dims, dtype)


def part(at, size):
    return pl.ds(pl.multiple_of(lax.rem(at, SIDE) * size, size), size)


def pairs_of(rows):
    side = rows // BLOCK
    return [(i, j) for i in range(side) for j in range(i + 1)]


def plan_kernel(owner_ref, grads_ref, table_ref, packed_ref, empty_ref):
    count = owner_ref.shape[0]

    def clear(g, _):
        table_ref[2, g] = -1
        table_ref[3, g] = 0
        return 0

    lax.fori_loop(0, count, clear, 0)

    def first(e, _):
        g = owner_ref[e]
        seen = table_ref[3, g]
        table_ref[3, g] = seen + 1

        @pl.when(seen == 0)
        def _():
            table_ref[0, g] = e
            table_ref[1, e] = g

        @pl.when(seen > 0)
        def _():
            table_ref[2, g] = e

        return 0

    lax.fori_loop(0, count, first, 0)

    def empties(g, n):
        none = table_ref[3, g] == 0

        @pl.when(none)
        def _():
            empty_ref[n] = g

        return n + none.astype(jnp.int32)

    lax.fori_loop(0, count, empties, 0)

    def second(g, n):
        e = table_ref[2, g]
        two = e >= 0

        @pl.when(two)
        def _():
            h = empty_ref[n]
            table_ref[2, g] = h
            table_ref[0, h] = e
            table_ref[1, e] = h

        return n + two.astype(jnp.int32)

    lax.fori_loop(0, count, second, 0)

    def move(g, _):
        packed_ref[g] = grads_ref[table_ref[0, g]]
        return 0

    lax.fori_loop(0, count, move, 0)


def plan(owner, grads):
    count = grads.shape[0]
    return pl.pallas_call(
        plan_kernel,
        out_shape=(shape_of(4, count, dtype=jnp.int32), shape_of(*grads.shape)),
        in_specs=[SMEM, VMEM],
        out_specs=(SMEM, VMEM),
        scratch_shapes=[pltpu.SMEM((count,), jnp.int32)],
        compiler_params=params(),
        name="plan",
    )(owner, grads)


def gram_kernel(pairs, squares, place_ref, x_ref, *refs):
    outs, full = refs[:SIDE], refs[-1]
    for t, (i, j) in enumerate(pairs):
        full[t] = lax.dot_general(
            x_ref[i * BLOCK : (i + 1) * BLOCK, :],
            x_ref[j * BLOCK : (j + 1) * BLOCK, :],
            (((1,), (1,)), ((), ())),
            preferred_element_type=jnp.float32,
        ).astype(jnp.bfloat16)
        for s in range(SIDE):
            outs[s][t] = full[t, part(place_ref[0] + s, PIECE), :]
    if squares:
        square_ref = refs[SIDE]
        total = jnp.zeros((1, x_ref.shape[1]), jnp.float32)
        for i in range(x_ref.shape[0] // BLOCK):
            values = x_ref[i * BLOCK : (i + 1) * BLOCK, :].astype(jnp.float32)
            total = total + jnp.sum(values * values, axis=0, keepdims=True)
        total = jnp.sum(total, axis=1, keepdims=True)
        square_ref[...] = jnp.broadcast_to(total, square_ref.shape)


def gram_terms(place, x, pairs, squares):
    out_shape = (shape_of(len(pairs), PIECE, BLOCK),) * SIDE
    if squares:
        out_shape += (shape_of(8, BLOCK, dtype=jnp.float32),)
    return pl.pallas_call(
        functools.partial(gram_kernel, pairs, squares),
        out_shape=out_shape,
        in_specs=[SMEM, VMEM],
        out_specs=(VMEM,) * len(out_shape),
        scratch_shapes=[pltpu.VMEM((len(pairs), BLOCK, BLOCK), jnp.bfloat16)],
        compiler_params=params(),
        cost_estimate=pl.CostEstimate(
            flops=2 * len(pairs) * BLOCK**3, bytes_accessed=4 * 1024 * 1024, transcendentals=0
        ),
        name="gram",
    )(place, x)


def split(number, shape):
    rest = jnp.broadcast_to(number, shape)
    row = lax.broadcasted_iota(jnp.int32, shape, 0)
    parts = jnp.zeros(shape, jnp.float32)
    for k in range(3):
        top = lax.reduce_precision(rest, 8, 7)
        parts = jnp.where(row == k, top, parts)
        rest = rest - top
    return parts.astype(jnp.bfloat16)


def add_kernel(blocks, squares, carried, *refs):
    ins, out = refs[:SIDE], refs[-1]
    total = ins[0][:blocks].astype(jnp.float32)
    for other in ins[1:]:
        total = total + other[:blocks].astype(jnp.float32)
    out[:blocks] = total.astype(jnp.bfloat16)
    if squares:
        out[blocks] = split(refs[SIDE][0:1, :], (PIECE, BLOCK))
    if carried:
        number = jnp.zeros((1, BLOCK), jnp.float32)
        for piece in ins:
            number = number + jnp.sum(piece[blocks].astype(jnp.float32), axis=0, keepdims=True)
        out[blocks] = split(number, (PIECE, BLOCK))


def add(pieces, square=None, carried=False):
    extra = () if square is None else (square,)
    blocks = pieces[0].shape[0] - carried
    return pl.pallas_call(
        functools.partial(add_kernel, blocks, square is not None, carried),
        out_shape=shape_of(blocks + (square is not None or carried), PIECE, BLOCK),
        in_specs=[VMEM] * (SIDE + len(extra)),
        out_specs=VMEM,
        compiler_params=params(),
        cost_estimate=pl.CostEstimate(
            flops=4 * blocks * PIECE * BLOCK, bytes_accessed=4 * 1024 * 1024, transcendentals=0
        ),
        name="add",
    )(*pieces, *extra)


def step_kernel(pairs, rows_all, factor, place_ref, x_ref, *refs):
    ins = refs[: 2 * SIDE]
    out_ref, gram, normed, left = refs[2 * SIDE :]
    blocks = ins[0].shape[0] - 1
    total = jnp.zeros((1, BLOCK), jnp.float32)
    for s in range(SIDE):
        total = total + jnp.sum(ins[s][blocks].astype(jnp.float32), axis=0, keepdims=True)
    inverse = 1.0 / jnp.sqrt(total / rows_all + 1e-06)
    scale = inverse * inverse
    side = rows_all // BLOCK
    for i in range(side):
        rows = slice(i * BLOCK, (i + 1) * BLOCK)
        normed[rows, :] = (x_ref[rows, :].astype(jnp.float32) * inverse).astype(jnp.bfloat16)
    for t, (i, j) in enumerate(pairs):
        source, u = (ins[:SIDE], t) if t < blocks else (ins[SIDE:], t - blocks)
        for s in range(SIDE):
            p = lax.rem(place_ref[0] - s + SIDE, SIDE)
            rows = pl.ds(pl.multiple_of(i * BLOCK + p * PIECE, PIECE), PIECE)
            values = source[s][u].astype(jnp.float32) * scale
            gram[rows, j * BLOCK : (j + 1) * BLOCK] = jnp.where(scale > 0, values, 0.0).astype(
                jnp.bfloat16
            )
    for i, j in pairs:
        if i != j:
            block = gram[i * BLOCK : (i + 1) * BLOCK, j * BLOCK : (j + 1) * BLOCK]
            gram[j * BLOCK : (j + 1) * BLOCK, i * BLOCK : (i + 1) * BLOCK] = block.T
    for i in range(side):
        rows = slice(i * BLOCK, (i + 1) * BLOCK)
        left[rows, :] = jnp.dot(
            gram[rows, :], normed[...], preferred_element_type=jnp.float32
        ).astype(jnp.bfloat16)
    for i in range(side):
        rows = slice(i * BLOCK, (i + 1) * BLOCK)
        right = jnp.dot(gram[rows, :], left[...], preferred_element_type=jnp.float32)
        mixed = (
            3.4445 * normed[rows, :].astype(jnp.float32)
            - 4.775 * left[rows, :].astype(jnp.float32)
            + 2.0315 * right
        )
        out_ref[rows, :] = (factor * mixed).astype(jnp.bfloat16)


def step(place, x, pieces, factor):
    rows, cols = x.shape
    pairs = pairs_of(rows)
    return pl.pallas_call(
        functools.partial(step_kernel, pairs, rows, factor),
        out_shape=shape_of(rows, cols),
        in_specs=[SMEM, VMEM] + [VMEM] * (2 * SIDE),
        out_specs=VMEM,
        scratch_shapes=[
            pltpu.VMEM((rows, rows), jnp.bfloat16),
            pltpu.VMEM((rows, cols), jnp.bfloat16),
            pltpu.VMEM((rows, cols), jnp.bfloat16),
        ],
        compiler_params=params(),
        name="step",
    )(place, x, *pieces)


def deal_kernel(table_ref, back_ref, update_ref, second_ref):
    count = back_ref.shape[0]

    def move(e, _):
        update_ref[e] = back_ref[table_ref[1, e]]
        helper = table_ref[2, e]
        block = back_ref[jnp.maximum(helper, 0)]
        second_ref[e] = jnp.where(helper >= 0, block, jnp.zeros_like(block))
        return 0

    lax.fori_loop(0, count, move, 0)


def deal(table, back):
    return pl.pallas_call(
        deal_kernel,
        out_shape=(shape_of(*back.shape),) * 2,
        in_specs=[SMEM, VMEM],
        out_specs=(VMEM,) * 2,
        compiler_params=params(),
        name="deal",
    )(table, back)


def spread(send, order):
    groups, places = lax.axis_size("fsdp"), SIDE * SIDE
    got = [send[0]]
    for amount in range(1, SIDE):
        moves = []
        for at in range(groups * places):
            group, place = divmod(at, places)
            y, x = divmod(place, SIDE)
            if group % 2 == order:
                x = (x + amount) % SIDE
            else:
                y = (y + amount) % SIDE
            moves.append((at, group * places + y * SIDE + x))
        got.append(lax.ppermute(send[amount], ("fsdp", "grp"), moves))
    return got


def on_device(grads, owner):
    count, rows_dev, cols_dev = grads.shape
    groups = lax.axis_size("fsdp")
    rows = rows_dev * groups
    cols = cols_dev * lax.axis_size("grp")
    factor = 0.2 * math.sqrt(max(rows, cols))
    at = lax.axis_index("grp")
    me = lax.axis_index("fsdp")
    along = jnp.stack([lax.rem(at, SIDE), lax.div(at, SIDE)]).astype(jnp.int32)
    place = jnp.where(lax.rem(me, 2) == 0, along, along[::-1])
    table, packed = plan(owner, grads)
    x = lax.all_to_all(packed, "fsdp", split_axis=0, concat_axis=0, tiled=True)
    x = x.reshape(rows, cols_dev)
    pairs = pairs_of(rows)
    cut = len(pairs) // 2
    *early, square = gram_terms(place, x, pairs[:cut], True)
    late = gram_terms(place, x, pairs[cut:], False)
    early = add(spread(early, 0), square)
    late = add(spread(late, 0))
    early = add(spread([early] * SIDE, 1), carried=True)
    late = add(spread([late] * SIDE, 1))
    pieces = spread([early] * SIDE, 0) + spread([late] * SIDE, 0)
    done = step(place, x, pieces, factor)
    back = lax.all_to_all(
        done.reshape(count, rows_dev, cols_dev), "fsdp", split_axis=0, concat_axis=0, tiled=True
    )
    update, second = deal(table, back)
    second = lax.all_to_all(second, "fsdp", split_axis=0, concat_axis=0, tiled=True)
    first = jnp.where(table[3, me] > 0, done, jnp.zeros_like(done))
    owned = jnp.stack([first, second.reshape(rows, cols_dev)], axis=0)
    return (update, owned)


def solution(mesh):
    return jax.shard_map(
        on_device,
        mesh=mesh,
        in_specs=(P(None, "fsdp", "grp"), P()),
        out_specs=(P(None, "fsdp", "grp"), P("fsdp", None, "grp")),
        check_vma=False,
    )
```

```python
import functools
import math

import jax
import jax.numpy as jnp
from jax import lax
from jax.experimental import pallas as pl
from jax.experimental.pallas import tpu as pltpu
from jax.sharding import PartitionSpec as P

MOST = 2
SIDE = 4
BLOCK = 256
PIECE = BLOCK // SIDE
VMEM_LIMIT = 56 * 1024 * 1024

VMEM = pl.BlockSpec(memory_space=pltpu.VMEM)
SMEM = pl.BlockSpec(memory_space=pltpu.SMEM)
ANY = pl.BlockSpec(memory_space=pl.ANY)


def params():
    return pltpu.CompilerParams(vmem_limit_bytes=VMEM_LIMIT)


def shape_of(*dims, dtype=jnp.bfloat16):
    return jax.ShapeDtypeStruct(dims, dtype)


def cost(flops, size):
    return pl.CostEstimate(flops=flops, bytes_accessed=size, transcendentals=0)


def part(at, size):
    return pl.ds(pl.multiple_of(lax.rem(at, SIDE) * size, size), size)


def pairs_of(rows):
    side = rows // BLOCK
    return [(i, j) for i in range(side) for j in range(i + 1)]


def move_all(moves, sems):
    copies = [pltpu.make_async_copy(a, b, sems.at[k]) for k, (a, b) in enumerate(moves)]
    for copy in copies:
        copy.start()
    for copy in copies:
        copy.wait()


def choose_all(moves, sems):
    copies = []
    for k, (choice, a, b, to) in enumerate(moves):
        yes = pltpu.make_async_copy(a, to, sems.at[k])
        no = pltpu.make_async_copy(b, to, sems.at[k])
        pl.when(choice)(yes.start)
        pl.when(jnp.logical_not(choice))(no.start)
        copies.append(yes)
    for copy in copies:
        copy.wait()


def group_at(spot_ref, away, other, planes):
    core = spot_ref[1]
    return 2 * lax.rem(spot_ref[0] + away, planes) + (1 - core if other else core)


def plan_kernel(owner_ref, spot_ref, grads_ref, table_ref, *refs):
    outs, empty_ref, sems = refs[:-2], refs[-2], refs[-1]
    count, planes = owner_ref.shape[0], len(outs)

    def clear(g, _):
        table_ref[1, g] = 0
        table_ref[2, g] = -1
        return 0

    lax.fori_loop(0, count, clear, 0)

    def first(e, _):
        g = owner_ref[e]
        seen = table_ref[1, g]
        table_ref[1, g] = seen + 1

        @pl.when(seen == 0)
        def _():
            table_ref[0, g] = e

        @pl.when(seen > 0)
        def _():
            table_ref[2, g] = e

        return 0

    lax.fori_loop(0, count, first, 0)

    def empties(g, n):
        none = table_ref[1, g] == 0

        @pl.when(none)
        def _():
            empty_ref[n] = g

        return n + none.astype(jnp.int32)

    lax.fori_loop(0, count, empties, 0)

    def second(g, n):
        e = table_ref[2, g]
        two = e >= 0

        @pl.when(two)
        def _():
            h = empty_ref[n]
            table_ref[2, g] = h
            table_ref[0, h] = e

        return n + two.astype(jnp.int32)

    lax.fori_loop(0, count, second, 0)
    moves = []
    for away in range(planes):
        for other in range(2):
            e = table_ref[0, group_at(spot_ref, away, other, planes)]
            moves.append((grads_ref.at[e], outs[away].at[other]))
    move_all(moves, sems)


def plan(owner, spot, grads):
    count, rows, cols = grads.shape
    planes = count // 2
    return pl.pallas_call(
        plan_kernel,
        out_shape=(shape_of(3, count, dtype=jnp.int32),) + (shape_of(2, rows, cols),) * planes,
        in_specs=[SMEM, SMEM, ANY],
        out_specs=(SMEM,) + (ANY,) * planes,
        scratch_shapes=[pltpu.SMEM((count,), jnp.int32), pltpu.SemaphoreType.DMA((count,))],
        compiler_params=params(),
        name="plan",
    )(owner, spot, grads)


def sort_kernel(*refs):
    ins, (own_ref, give_ref, sems) = refs[:-3], refs[-3:]
    moves = [(ref.at[0], own_ref.at[k]) for k, ref in enumerate(ins)]
    moves += [(ref.at[1], give_ref.at[k]) for k, ref in enumerate(ins)]
    move_all(moves, sems)


def sort(blocks):
    planes = len(blocks)
    _, rows, cols = blocks[0].shape
    return pl.pallas_call(
        sort_kernel,
        out_shape=(shape_of(planes, rows, cols),) * 2,
        in_specs=[ANY] * planes,
        out_specs=(ANY,) * 2,
        scratch_shapes=[pltpu.SemaphoreType.DMA((2 * planes,))],
        compiler_params=params(),
        name="sort",
    )(*blocks)


def split(number, shape):
    rest = jnp.broadcast_to(number, shape)
    row = lax.broadcasted_iota(jnp.int32, shape, 0)
    parts = jnp.zeros(shape, jnp.float32)
    for k in range(3):
        top = lax.reduce_precision(rest, 8, 7)
        parts = jnp.where(row == k, top, parts)
        rest = rest - top
    return parts.astype(jnp.bfloat16)


def gram_kernel(low, squares, place_ref, *refs):
    lists = [refs[k : k + SIDE] for k in range(0, len(refs) - 2, SIDE)]
    out_ref, picked = refs[-2:]
    each = lists[0][0].shape[0] // BLOCK
    side = each * len(lists)
    rows = part(place_ref[0], PIECE)

    def block(s, i):
        start = (i % each) * BLOCK
        return lists[i // each][s][start : start + BLOCK, :]

    for s in range(SIDE):
        for i in range(low, side):
            start = pl.multiple_of((i % each) * BLOCK + lax.rem(place_ref[0], SIDE) * PIECE, PIECE)
            picked[s, (i - low) * PIECE : (i - low + 1) * PIECE, :] = lists[i // each][s][
                pl.ds(start, PIECE), :
            ]
    index = {pair: t for t, pair in enumerate(p for p in pairs_of(side * BLOCK) if p[0] >= low)}
    for j in range(side):
        top = max(j, low)
        total = jnp.zeros(((side - top) * PIECE, BLOCK), jnp.float32)
        for s in range(SIDE):
            total = total + lax.dot_general(
                picked[s, (top - low) * PIECE :, :],
                block(s, j),
                (((1,), (1,)), ((), ())),
                preferred_element_type=jnp.float32,
            )
        total = total.astype(jnp.bfloat16)
        for i in range(top, side):
            out_ref[index[i, j]] = total[(i - top) * PIECE : (i - top + 1) * PIECE, :]
    if squares:
        total = jnp.zeros((1, BLOCK), jnp.float32)
        for i in range(side):
            values = block(0, i).astype(jnp.float32)
            total = total + jnp.sum(values * values, axis=0, keepdims=True)
        total = jnp.sum(total, axis=1, keepdims=True)
        out_ref[len(index)] = split(total, (PIECE, BLOCK))


def gram_quarter(place, lists, low, squares):
    side = len(lists) * lists[0][0].shape[0] // BLOCK
    blocks = len([p for p in pairs_of(side * BLOCK) if p[0] >= low])
    return pl.pallas_call(
        functools.partial(gram_kernel, low, squares),
        out_shape=shape_of(blocks + squares, PIECE, BLOCK),
        in_specs=[SMEM] + [VMEM] * (SIDE * len(lists)),
        out_specs=VMEM,
        scratch_shapes=[pltpu.VMEM((SIDE, (side - low) * PIECE, BLOCK), jnp.bfloat16)],
        compiler_params=params(),
        cost_estimate=cost(2 * blocks * BLOCK**3, 4 * 1024 * 1024),
        name="gram",
    )(place, *[x for xs in lists for x in xs])


def add_kernel(blocks, carried, *refs):
    ins, out = refs[:SIDE], refs[-1]
    total = ins[0][:blocks].astype(jnp.float32)
    for other in ins[1:]:
        total = total + other[:blocks].astype(jnp.float32)
    out[:blocks] = total.astype(jnp.bfloat16)
    if carried:
        number = jnp.zeros((1, BLOCK), jnp.float32)
        for piece in ins:
            number = number + jnp.sum(piece[blocks].astype(jnp.float32), axis=0, keepdims=True)
        out[blocks] = split(number, (PIECE, BLOCK))


def add(pieces, carried):
    blocks = pieces[0].shape[0] - carried
    return pl.pallas_call(
        functools.partial(add_kernel, blocks, carried),
        out_shape=shape_of(blocks + carried, PIECE, BLOCK),
        in_specs=[VMEM] * SIDE,
        out_specs=VMEM,
        compiler_params=params(),
        cost_estimate=cost(4 * blocks * PIECE * BLOCK, 4 * 1024 * 1024),
        name="add",
    )(*pieces)


def step_kernel(pairs, factor, planes, place_ref, own_ref, got_ref, *refs):
    early, late = refs[:SIDE], refs[SIDE : 2 * SIDE]
    outs, (gram, normed, left) = refs[2 * SIDE : -3], refs[-3:]
    half = own_ref.shape[0]
    blocks = early[0].shape[0]
    total = jnp.zeros((1, BLOCK), jnp.float32)
    for s in range(SIDE):
        total = total + jnp.sum(
            late[s][len(pairs) - blocks].astype(jnp.float32), axis=0, keepdims=True
        )
    inverse = 1.0 / jnp.sqrt(total / (2 * half) + 1e-06)
    scale = inverse * inverse
    side = 2 * half // BLOCK
    for k, ref in enumerate((own_ref, got_ref)):
        for i in range(half // BLOCK):
            values = ref[i * BLOCK : (i + 1) * BLOCK, :].astype(jnp.float32) * inverse
            normed[k * half + i * BLOCK : k * half + (i + 1) * BLOCK, :] = values.astype(
                jnp.bfloat16
            )
    for t, (i, j) in enumerate(pairs):
        source, u = (early, t) if t < blocks else (late, t - blocks)
        for s in range(SIDE):
            p = lax.rem(place_ref[0] - s + SIDE, SIDE)
            rows = pl.ds(pl.multiple_of(i * BLOCK + p * PIECE, PIECE), PIECE)
            values = source[s][u].astype(jnp.float32) * scale
            gram[rows, j * BLOCK : (j + 1) * BLOCK] = jnp.where(scale > 0, values, 0.0).astype(
                jnp.bfloat16
            )
    for i, j in pairs:
        if i != j:
            block = gram[i * BLOCK : (i + 1) * BLOCK, j * BLOCK : (j + 1) * BLOCK]
            gram[j * BLOCK : (j + 1) * BLOCK, i * BLOCK : (i + 1) * BLOCK] = block.T
    for i in range(side):
        rows = slice(i * BLOCK, (i + 1) * BLOCK)
        left[rows, :] = jnp.dot(
            gram[rows, :], normed[...], preferred_element_type=jnp.float32
        ).astype(jnp.bfloat16)
    each = half // planes
    for k in range(2):
        for away in range(0, planes, 2):
            rows = slice(k * half + away * each, k * half + (away + 2) * each)
            right = jnp.dot(gram[rows, :], left[...], preferred_element_type=jnp.float32)
            mixed = (
                3.4445 * normed[rows, :].astype(jnp.float32)
                - 4.775 * left[rows, :].astype(jnp.float32)
                + 2.0315 * right
            )
            values = (factor * mixed).astype(jnp.bfloat16)
            outs[away][k] = values[:each]
            outs[away + 1][k] = values[each:]


def step(place, own, got, early, late, factor, planes):
    half, cols = own.shape
    rows = 2 * half
    return pl.pallas_call(
        functools.partial(step_kernel, pairs_of(rows), factor, planes),
        out_shape=(shape_of(2, half // planes, cols),) * planes,
        in_specs=[SMEM] + [VMEM] * (2 + 2 * SIDE),
        out_specs=(VMEM,) * planes,
        scratch_shapes=[
            pltpu.VMEM((rows, rows), jnp.bfloat16),
            pltpu.VMEM((rows, cols), jnp.bfloat16),
            pltpu.VMEM((rows, cols), jnp.bfloat16),
        ],
        compiler_params=params(),
        cost_estimate=cost(4 * rows * rows * cols, 6 * 1024 * 1024),
        name="step",
    )(place, own, got, *early, *late)


def helper_of(table_ref, spot_ref, group, planes):
    helper = table_ref[2, group]
    there = helper >= 0
    helper = jnp.maximum(helper, 0)
    mine = jnp.logical_and(there, lax.rem(helper, 2) == spot_ref[1])
    return there, mine, lax.rem(lax.div(helper, 2) - spot_ref[0] + planes, planes)


def pick_kernel(planes, table_ref, spot_ref, *refs):
    ins = refs[:planes]
    mine_ref, give_ref, rest_ref, held, sems = refs[planes:]
    move_all([(ref, held.at[k]) for k, ref in enumerate(ins)], sems)
    moves = [(held.at[k, 1], rest_ref.at[k]) for k in range(planes)]
    for away in range(planes):
        for other, out in enumerate((mine_ref, give_ref)):
            group = group_at(spot_ref, away, other, planes)
            _, mine, up = helper_of(table_ref, spot_ref, group, planes)
            moves.append((held.at[jnp.where(mine, up, planes)], out.at[away]))
    held[planes] = jnp.zeros(held.shape[1:], held.dtype)
    move_all(moves, sems)


def pick(table, spot, back):
    planes = len(back)
    block = back[0].shape
    return pl.pallas_call(
        functools.partial(pick_kernel, planes),
        out_shape=(shape_of(planes, *block),) * 2 + (shape_of(planes, *block[1:]),),
        in_specs=[SMEM] * 2 + [ANY] * planes,
        out_specs=(ANY,) * 3,
        scratch_shapes=[
            pltpu.VMEM((planes + 1, *block), jnp.bfloat16),
            pltpu.SemaphoreType.DMA((3 * planes,)),
        ],
        compiler_params=params(),
        name="pick",
    )(table, spot, *back)


def merge_kernel(planes, table_ref, spot_ref, mine_ref, got_ref, *refs):
    outs, sems = refs[:planes], refs[planes]
    moves = []
    for away in range(planes):
        group = group_at(spot_ref, away, 0, planes)
        there, mine, _ = helper_of(table_ref, spot_ref, group, planes)
        here = jnp.logical_or(mine, jnp.logical_not(there))
        for k in range(2):
            moves.append((here, mine_ref.at[away, k], got_ref.at[away, 1 - k], outs[away].at[k]))
    choose_all(moves, sems)


def merge(table, spot, mine, got):
    planes = mine.shape[0]
    return pl.pallas_call(
        functools.partial(merge_kernel, planes),
        out_shape=(shape_of(*mine.shape[1:]),) * planes,
        in_specs=[SMEM] * 2 + [ANY] * 2,
        out_specs=(ANY,) * planes,
        scratch_shapes=[pltpu.SemaphoreType.DMA((2 * planes,))],
        compiler_params=params(),
        name="merge",
    )(table, spot, mine, got)


def update_kernel(planes, table_ref, spot_ref, *refs):
    ins, rest_ref, out_ref, sems = refs[:planes], *refs[planes:]
    moves = []
    for away in range(planes):
        e = table_ref[0, group_at(spot_ref, away, 0, planes)]
        moves.append((ins[away].at[0], out_ref.at[e]))
        e = table_ref[0, group_at(spot_ref, away, 1, planes)]
        moves.append((rest_ref.at[away], out_ref.at[e]))
    move_all(moves, sems)


def update_of(table, spot, back, rest):
    planes, rows, cols = rest.shape
    return pl.pallas_call(
        functools.partial(update_kernel, planes),
        out_shape=shape_of(2 * planes, rows, cols),
        in_specs=[SMEM] * 2 + [ANY] * (planes + 1),
        out_specs=ANY,
        scratch_shapes=[pltpu.SemaphoreType.DMA((2 * planes,))],
        compiler_params=params(),
        name="update",
    )(table, spot, *back, rest)


def slot_moves(spot_ref, ins, out_ref, slot):
    planes = len(ins)
    moves = []
    for away, ref in enumerate(ins):
        for k in range(2):
            rows = ref.shape[1]
            start = group_at(spot_ref, planes - away, k, planes) * rows
            to = out_ref.at[slot, pl.ds(pl.multiple_of(start, rows), rows)]
            moves.append((ref.at[k], to))
    return moves


def first_kernel(planes, table_ref, spot_ref, *refs):
    ins, out_ref, zero, sems = refs[:planes], *refs[planes:]
    zero[...] = jnp.zeros(zero.shape, zero.dtype)
    owns = table_ref[1, group_at(spot_ref, 0, 0, planes)] > 0
    moves = slot_moves(spot_ref, ins, out_ref, 0)
    choose_all([(owns, a, zero, b) for a, b in moves], sems)


def second_kernel(planes, spot_ref, *refs):
    ins, _, out_ref, sems = refs[:planes], *refs[planes:]
    move_all(slot_moves(spot_ref, ins, out_ref, 1), sems)


def first_slot(table, spot, done):
    planes = len(done)
    _, rows, cols = done[0].shape
    return pl.pallas_call(
        functools.partial(first_kernel, planes),
        out_shape=shape_of(MOST, 2 * planes * rows, cols),
        in_specs=[SMEM] * 2 + [ANY] * planes,
        out_specs=ANY,
        scratch_shapes=[
            pltpu.VMEM((rows, cols), jnp.bfloat16),
            pltpu.SemaphoreType.DMA((2 * planes,)),
        ],
        compiler_params=params(),
        name="first_slot",
    )(table, spot, *done)


def second_slot(spot, came, owned):
    planes = len(came)
    return pl.pallas_call(
        functools.partial(second_kernel, planes),
        out_shape=shape_of(*owned.shape),
        in_specs=[SMEM] + [ANY] * (planes + 1),
        out_specs=ANY,
        scratch_shapes=[pltpu.SemaphoreType.DMA((2 * planes,))],
        input_output_aliases={planes + 1: 0},
        compiler_params=params(),
        name="second_slot",
    )(spot, *came, owned)


def spread(value, order):
    groups, places = lax.axis_size("fsdp"), SIDE * SIDE
    got = [value] * SIDE
    for amount in (1, 3, 2):
        moves = []
        for at in range(groups * places):
            group, place = divmod(at, places)
            y, x = divmod(place, SIDE)
            if group % 2 == order:
                x = (x + amount) % SIDE
            else:
                y = (y + amount) % SIDE
            moves.append((at, group * places + y * SIDE + x))
        got[amount] = lax.ppermute(value, ("fsdp", "grp"), moves)
    return got


def over_planes(blocks, sign):
    planes = len(blocks)
    got = list(blocks)
    for away in sorted(range(1, planes), key=lambda a: -min(a, planes - a)):
        moves = []
        for group in range(2 * planes):
            plane, core = divmod(group, 2)
            moves.append((group, 2 * ((plane + sign * away) % planes) + core))
        got[away] = lax.ppermute(blocks[away], "fsdp", moves)
    return got


def swap(value):
    groups = lax.axis_size("fsdp")
    return lax.ppermute(value, "fsdp", [(g, g ^ 1) for g in range(groups)])


def on_device(grads, owner):
    count, rows_dev, cols_dev = grads.shape
    groups = lax.axis_size("fsdp")
    planes = groups // 2
    rows = rows_dev * groups
    cols = cols_dev * lax.axis_size("grp")
    factor = 0.2 * math.sqrt(max(rows, cols))
    at = lax.axis_index("grp")
    me = lax.axis_index("fsdp")
    along = jnp.stack([lax.rem(at, SIDE), lax.div(at, SIDE)]).astype(jnp.int32)
    place = jnp.where(lax.rem(me, 2) == 0, along, along[::-1])
    spot = jnp.stack([lax.div(me, 2), lax.rem(me, 2)]).astype(jnp.int32)
    table, *sends = plan(owner, spot, grads)
    own, give = sort(over_planes(sends, 1))
    got = swap(give)
    own, got = own.reshape(rows // 2, cols_dev), got.reshape(rows // 2, cols_dev)
    owns, gots = spread(own, 0), spread(got, 0)
    early = gram_quarter(place, [owns], 0, False)
    late = gram_quarter(place, [owns, gots], rows // 2 // BLOCK, True)
    early = add(spread(early, 1), False)
    late = add(spread(late, 1), True)
    done = step(place, own, got, spread(early, 0), spread(late, 0), factor, planes)
    back = over_planes(done, -1)
    mine, give, rest = pick(table, spot, back)
    sends = merge(table, spot, mine, swap(give))
    came = over_planes(sends, 1)
    update = update_of(table, spot, back, swap(rest))
    owned = second_slot(spot, came, first_slot(table, spot, done))
    return (update, owned)


def solution(mesh):
    return jax.shard_map(
        on_device,
        mesh=mesh,
        in_specs=(P(None, "fsdp", "grp"), P()),
        out_specs=(P(None, "fsdp", "grp"), P("fsdp", None, "grp")),
        check_vma=False,
    )
```

```python
import functools
import math

import jax
import jax.numpy as jnp
from jax import lax
from jax.experimental import pallas as pl
from jax.experimental.pallas import tpu as pltpu
from jax.sharding import PartitionSpec as P

MOST = 2
SIDE = 4
BLOCK = 256
PIECE = BLOCK // SIDE
MIB = 1024 * 1024

VMEM = pl.BlockSpec(memory_space=pltpu.VMEM)
SMEM = pl.BlockSpec(memory_space=pltpu.SMEM)
ANY = pl.BlockSpec(memory_space=pl.ANY)


def params(mib):
    return pltpu.CompilerParams(vmem_limit_bytes=mib * MIB)


def shape_of(*dims, dtype=jnp.bfloat16):
    return jax.ShapeDtypeStruct(dims, dtype)


def cost(flops, size):
    return pl.CostEstimate(flops=flops, bytes_accessed=size, transcendentals=0)


def part(at, size):
    return pl.ds(pl.multiple_of(lax.rem(at, SIDE) * size, size), size)


def pairs_of(rows):
    side = rows // BLOCK
    return [(i, j) for i in range(side) for j in range(i + 1)]


def move_all(moves, sems):
    copies = [pltpu.make_async_copy(a, b, sems.at[k]) for k, (a, b) in enumerate(moves)]
    for copy in copies:
        copy.start()
    for copy in copies:
        copy.wait()


def group_at(spot_ref, away, other, planes):
    core = spot_ref[1]
    return 2 * lax.rem(spot_ref[0] + away, planes) + (1 - core if other else core)


def plan_kernel(owner_ref, spot_ref, grads_ref, table_ref, *refs):
    outs, empty_ref = refs[:-1], refs[-1]
    count, planes = owner_ref.shape[0], len(outs)

    def clear(g, _):
        table_ref[1, g] = 0
        table_ref[2, g] = -1
        table_ref[3, g] = -1
        return 0

    lax.fori_loop(0, count, clear, 0)

    def first(e, _):
        g = owner_ref[e]
        seen = table_ref[1, g]
        table_ref[1, g] = seen + 1

        @pl.when(seen == 0)
        def _():
            table_ref[0, g] = e

        @pl.when(seen > 0)
        def _():
            table_ref[2, g] = e

        return 0

    lax.fori_loop(0, count, first, 0)

    def empties(g, n):
        none = table_ref[1, g] == 0

        @pl.when(none)
        def _():
            empty_ref[n] = g

        return n + none.astype(jnp.int32)

    lax.fori_loop(0, count, empties, 0)

    def second(g, n):
        e = table_ref[2, g]
        two = e >= 0

        @pl.when(two)
        def _():
            h = empty_ref[n]
            table_ref[2, g] = h
            table_ref[0, h] = e
            table_ref[3, h] = g

        return n + two.astype(jnp.int32)

    lax.fori_loop(0, count, second, 0)
    for away in range(planes):
        for other in range(2):
            outs[away][other] = grads_ref[table_ref[0, group_at(spot_ref, away, other, planes)]]


def plan(owner, spot, grads):
    count, rows, cols = grads.shape
    planes = count // 2
    return pl.pallas_call(
        plan_kernel,
        out_shape=(shape_of(4, count, dtype=jnp.int32),) + (shape_of(2, rows, cols),) * planes,
        in_specs=[SMEM, SMEM, VMEM],
        out_specs=(SMEM,) + (VMEM,) * planes,
        scratch_shapes=[pltpu.SMEM((count,), jnp.int32)],
        compiler_params=params(8),
        name="plan",
    )(owner, spot, grads)


def sort_kernel(*refs):
    ins, (own_ref, give_ref) = in_place(refs[:-2]), refs[-2:]
    for k, ref in enumerate(ins):
        own_ref[k] = ref[0]
        give_ref[k] = ref[1]


def sort(blocks):
    planes = len(blocks)
    _, rows, cols = blocks[0].shape
    return pl.pallas_call(
        sort_kernel,
        out_shape=(shape_of(planes, rows, cols),) * 2,
        in_specs=[VMEM] * planes,
        out_specs=(VMEM,) * 2,
        compiler_params=params(8),
        name="sort",
    )(*in_turn(blocks))


def split(number, shape):
    rest = jnp.broadcast_to(number, shape)
    row = lax.broadcasted_iota(jnp.int32, shape, 0)
    parts = jnp.zeros(shape, jnp.float32)
    for k in range(3):
        top = lax.reduce_precision(rest, 8, 7)
        parts = jnp.where(row == k, top, parts)
        rest = rest - top
    return parts.astype(jnp.bfloat16)


def gram_kernel(place_ref, *refs):
    lists = in_lists(refs[: 2 * SIDE])
    *outs, picked = refs[2 * SIDE :]
    each = lists[0][0].shape[0] // BLOCK
    side = 2 * each
    turn = lax.rem(place_ref[0], SIDE) * PIECE

    def block(s, i):
        start = (i % each) * BLOCK
        return lists[i // each][s][start : start + BLOCK, :]

    for s in range(SIDE):
        for i in range(side):
            start = pl.multiple_of((i % each) * BLOCK + turn, PIECE)
            picked[s, i * PIECE : (i + 1) * PIECE, :] = lists[i // each][s][pl.ds(start, PIECE), :]
    index = {pair: t for t, pair in enumerate(pairs_of(side * BLOCK))}
    cut = outs[0].shape[0]
    for j in range(side):
        total = jnp.zeros(((side - j) * PIECE, BLOCK), jnp.float32)
        for s in range(SIDE):
            total = total + lax.dot_general(
                picked[s, j * PIECE :, :],
                block(s, j),
                (((1,), (1,)), ((), ())),
                preferred_element_type=jnp.float32,
            )
        total = total.astype(jnp.bfloat16)
        for i in range(j, side):
            t = index[i, j]
            outs[t // cut][t % cut] = total[(i - j) * PIECE : (i - j + 1) * PIECE, :]
    total = jnp.zeros((1, BLOCK), jnp.float32)
    for i in range(side):
        values = block(0, i).astype(jnp.float32)
        total = total + jnp.sum(values * values, axis=0, keepdims=True)
    total = jnp.sum(total, axis=1, keepdims=True)
    outs[1][outs[1].shape[0] - 1] = split(total, (PIECE, BLOCK))


def gram_quarter(place, lists):
    rows = 2 * lists[0][0].shape[0]
    blocks = len(pairs_of(rows))
    cut = (blocks + 1) // 2
    return pl.pallas_call(
        gram_kernel,
        out_shape=(shape_of(cut, PIECE, BLOCK), shape_of(blocks + 1 - cut, PIECE, BLOCK)),
        in_specs=[SMEM] + [VMEM] * (2 * SIDE),
        out_specs=(VMEM,) * 2,
        scratch_shapes=[pltpu.VMEM((SIDE, rows // SIDE, BLOCK), jnp.bfloat16)],
        compiler_params=params(16),
        cost_estimate=cost(2 * blocks * BLOCK**3, 4 * MIB),
        name="gram",
    )(place, *out_of_lists(lists))


def add_kernel(*refs):
    lists, outs = in_lists(refs[: 2 * SIDE]), refs[2 * SIDE :]
    for ins, out in zip(lists, outs):
        total = ins[0][...].astype(jnp.float32)
        for other in ins[1:]:
            total = total + other[...].astype(jnp.float32)
        out[...] = total.astype(jnp.bfloat16)
    last = outs[1].shape[0] - 1
    number = jnp.zeros((1, BLOCK), jnp.float32)
    for piece in lists[1]:
        number = number + jnp.sum(piece[last].astype(jnp.float32), axis=0, keepdims=True)
    outs[1][last] = split(number, (PIECE, BLOCK))


def add(lists):
    return pl.pallas_call(
        add_kernel,
        out_shape=tuple(shape_of(*pieces[0].shape) for pieces in lists),
        in_specs=[VMEM] * (2 * SIDE),
        out_specs=(VMEM,) * 2,
        compiler_params=params(12),
        name="add",
    )(*out_of_lists(lists))


def step_kernel(pairs, factor, planes, place_ref, own_ref, got_ref, *refs):
    early, late = in_lists(refs[: 2 * SIDE])
    outs, (gram, normed, left) = refs[2 * SIDE : -3], refs[-3:]
    half = own_ref.shape[0]
    blocks = early[0].shape[0]
    total = jnp.zeros((1, BLOCK), jnp.float32)
    for s in range(SIDE):
        total = total + jnp.sum(
            late[s][len(pairs) - blocks].astype(jnp.float32), axis=0, keepdims=True
        )
    inverse = 1.0 / jnp.sqrt(total / (2 * half) + 1e-06)
    scale = inverse * inverse
    side = 2 * half // BLOCK
    for k, ref in enumerate((own_ref, got_ref)):
        for i in range(half // BLOCK):
            values = ref[i * BLOCK : (i + 1) * BLOCK, :].astype(jnp.float32) * inverse
            normed[k * half + i * BLOCK : k * half + (i + 1) * BLOCK, :] = values.astype(
                jnp.bfloat16
            )
    for t, (i, j) in enumerate(pairs):
        source, u = (early, t) if t < blocks else (late, t - blocks)
        for s in range(SIDE):
            p = lax.rem(place_ref[0] - s + SIDE, SIDE)
            rows = pl.ds(pl.multiple_of(i * BLOCK + p * PIECE, PIECE), PIECE)
            values = source[s][u].astype(jnp.float32) * scale
            gram[rows, j * BLOCK : (j + 1) * BLOCK] = jnp.where(scale > 0, values, 0.0).astype(
                jnp.bfloat16
            )
    for i, j in pairs:
        if i != j:
            block = gram[i * BLOCK : (i + 1) * BLOCK, j * BLOCK : (j + 1) * BLOCK]
            gram[j * BLOCK : (j + 1) * BLOCK, i * BLOCK : (i + 1) * BLOCK] = block.T
    for i in range(side):
        rows = slice(i * BLOCK, (i + 1) * BLOCK)
        left[rows, :] = jnp.dot(
            gram[rows, :], normed[...], preferred_element_type=jnp.float32
        ).astype(jnp.bfloat16)
    each = half // planes
    for k in range(2):
        for away in range(0, planes, 2):
            rows = slice(k * half + away * each, k * half + (away + 2) * each)
            right = jnp.dot(gram[rows, :], left[...], preferred_element_type=jnp.float32)
            mixed = (
                3.4445 * normed[rows, :].astype(jnp.float32)
                - 4.775 * left[rows, :].astype(jnp.float32)
                + 2.0315 * right
            )
            values = (factor * mixed).astype(jnp.bfloat16)
            outs[away][k] = values[:each]
            outs[away + 1][k] = values[each:]


def step(place, own, got, lists, factor, planes):
    half, cols = own.shape
    rows = 2 * half
    return pl.pallas_call(
        functools.partial(step_kernel, pairs_of(rows), factor, planes),
        out_shape=(shape_of(2, half // planes, cols),) * planes,
        in_specs=[SMEM] + [VMEM] * (2 + 2 * SIDE),
        out_specs=(VMEM,) * planes,
        scratch_shapes=[
            pltpu.VMEM((rows, rows), jnp.bfloat16),
            pltpu.VMEM((rows, cols), jnp.bfloat16),
            pltpu.VMEM((rows, cols), jnp.bfloat16),
        ],
        compiler_params=params(28),
        cost_estimate=cost(4 * rows * rows * cols, 6 * 1024 * 1024),
        name="step",
    )(place, own, got, *out_of_lists(lists))


def pick_kernel(planes, table_ref, spot_ref, *refs):
    ins, (mine_ref, give_ref, rest_ref) = in_place(refs[:planes]), refs[planes:]
    for up, ref in enumerate(ins):
        owner = table_ref[3, group_at(spot_ref, up, 0, planes)]
        away = lax.rem(lax.div(jnp.maximum(owner, 0), 2) - spot_ref[0] + planes, planes)
        here = lax.rem(jnp.maximum(owner, 0), 2) == spot_ref[1]

        @pl.when(jnp.logical_and(owner >= 0, here))
        def _():
            mine_ref[away] = ref[...]

        @pl.when(jnp.logical_and(owner >= 0, jnp.logical_not(here)))
        def _():
            give_ref[away] = ref[...]

        rest_ref[up] = ref[1]


def pick(table, spot, back):
    planes = len(back)
    block = back[0].shape
    return pl.pallas_call(
        functools.partial(pick_kernel, planes),
        out_shape=(shape_of(planes, *block),) * 2 + (shape_of(planes, *block[1:]),),
        in_specs=[SMEM] * 2 + [VMEM] * planes,
        out_specs=(VMEM,) * 3,
        compiler_params=params(8),
        name="pick",
    )(table, spot, *in_turn(back))


def merge_kernel(planes, table_ref, spot_ref, mine_ref, got_ref, *outs):
    for away, out in enumerate(outs):
        helper = table_ref[2, group_at(spot_ref, away, 0, planes)]
        here = lax.rem(jnp.maximum(helper, 0), 2) == spot_ref[1]

        @pl.when(helper < 0)
        def _():
            out[...] = jnp.zeros(out.shape, out.dtype)

        @pl.when(jnp.logical_and(helper >= 0, here))
        def _():
            out[...] = mine_ref[away]

        @pl.when(jnp.logical_and(helper >= 0, jnp.logical_not(here)))
        def _():
            out[0] = got_ref[away, 1]
            out[1] = got_ref[away, 0]


def merge(table, spot, mine, got):
    planes = mine.shape[0]
    return pl.pallas_call(
        functools.partial(merge_kernel, planes),
        out_shape=(shape_of(*mine.shape[1:]),) * planes,
        in_specs=[SMEM] * 2 + [VMEM] * 2,
        out_specs=(VMEM,) * planes,
        compiler_params=params(8),
        name="merge",
    )(table, spot, mine, got)


def update_kernel(planes, table_ref, spot_ref, *refs):
    ins, (rest_ref, out_ref, sems) = in_place(refs[:planes]), refs[planes:]
    moves = []
    for away in range(planes):
        e = table_ref[0, group_at(spot_ref, away, 0, planes)]
        moves.append((ins[away].at[0], out_ref.at[e]))
        e = table_ref[0, group_at(spot_ref, away, 1, planes)]
        moves.append((rest_ref.at[away], out_ref.at[e]))
    move_all(moves, sems)


def update_of(table, spot, back, rest):
    planes, rows, cols = rest.shape
    return pl.pallas_call(
        functools.partial(update_kernel, planes),
        out_shape=shape_of(2 * planes, rows, cols),
        in_specs=[SMEM] * 2 + [VMEM] * (planes + 1),
        out_specs=ANY,
        scratch_shapes=[pltpu.SemaphoreType.DMA((2 * planes,))],
        compiler_params=params(8),
        name="update",
    )(table, spot, *in_turn(back), rest)


def slot_moves(spot_ref, ins, out_ref, slot):
    planes = len(ins)
    moves = []
    for away, ref in enumerate(ins):
        for k in range(2):
            rows = ref.shape[1]
            start = group_at(spot_ref, planes - away, k, planes) * rows
            to = out_ref.at[slot, pl.ds(pl.multiple_of(start, rows), rows)]
            moves.append((ref.at[k], to))
    return moves


def first_kernel(planes, table_ref, spot_ref, *refs):
    ins, (out_ref, zero, sems) = refs[:planes], refs[planes:]
    moves = slot_moves(spot_ref, ins, out_ref, 0)
    owns = table_ref[1, group_at(spot_ref, 0, 0, planes)] > 0

    @pl.when(owns)
    def _():
        move_all(moves, sems)

    @pl.when(jnp.logical_not(owns))
    def _():
        zero[...] = jnp.zeros(zero.shape, zero.dtype)
        move_all([(zero, b) for _, b in moves], sems)


def second_kernel(planes, spot_ref, *refs):
    ins, (_, out_ref, sems) = in_place(refs[:planes]), refs[planes:]
    move_all(slot_moves(spot_ref, ins, out_ref, 1), sems)


def first_slot(table, spot, done):
    planes = len(done)
    _, rows, cols = done[0].shape
    return pl.pallas_call(
        functools.partial(first_kernel, planes),
        out_shape=shape_of(MOST, 2 * planes * rows, cols),
        in_specs=[SMEM] * 2 + [VMEM] * planes,
        out_specs=ANY,
        scratch_shapes=[
            pltpu.VMEM((rows, cols), jnp.bfloat16),
            pltpu.SemaphoreType.DMA((2 * planes,)),
        ],
        compiler_params=params(8),
        name="first_slot",
    )(table, spot, *done)


def second_slot(spot, came, owned):
    planes = len(came)
    return pl.pallas_call(
        functools.partial(second_kernel, planes),
        out_shape=shape_of(*owned.shape),
        in_specs=[SMEM] + [VMEM] * planes + [ANY],
        out_specs=ANY,
        scratch_shapes=[pltpu.SemaphoreType.DMA((2 * planes,))],
        input_output_aliases={planes + 1: 0},
        compiler_params=params(8),
        name="second_slot",
    )(spot, *in_turn(came), owned)


def neighbour(value, order, amount):
    groups, places = lax.axis_size("fsdp"), SIDE * SIDE
    moves = []
    for at in range(groups * places):
        group, place = divmod(at, places)
        y, x = divmod(place, SIDE)
        if group % 2 == order:
            x = (x + amount) % SIDE
        else:
            y = (y + amount) % SIDE
        moves.append((at, group * places + y * SIDE + x))
    return lax.ppermute(value, ("fsdp", "grp"), moves)


def gather(first, second, order):
    one = [first, neighbour(first, order, 1), None, neighbour(first, order, -1)]
    two = [second, neighbour(second, order, 1), None, neighbour(second, order, -1)]
    one[2] = neighbour(one[1], order, 1)
    two[2] = neighbour(two[3], order, -1)
    return one, two


TRAVEL = ((0, 0), (1, 0), (0, 1), (1, 3), (0, 3), (1, 1), (0, 2), (1, 2))


def out_of_lists(lists):
    return [lists[k][s] for k, s in TRAVEL]


def in_lists(refs):
    return [[refs[TRAVEL.index((k, s))] for s in range(SIDE)] for k in range(2)]


def over_planes(blocks, sign):
    planes = len(blocks)
    got = list(blocks)
    for away in nearest_first(planes)[1:]:
        moves = []
        for group in range(2 * planes):
            plane, core = divmod(group, 2)
            moves.append((group, 2 * ((plane + sign * away) % planes) + core))
        got[away] = lax.ppermute(blocks[away], "fsdp", moves)
    return got


def nearest_first(planes):
    return sorted(range(planes), key=lambda a: min(a, planes - a))


def in_turn(blocks):
    return [blocks[away] for away in nearest_first(len(blocks))]


def in_place(refs):
    order = nearest_first(len(refs))
    return [refs[order.index(away)] for away in range(len(refs))]


def swap(value):
    groups = lax.axis_size("fsdp")
    return lax.ppermute(value, "fsdp", [(g, g ^ 1) for g in range(groups)])


def on_device(grads, owner):
    count, rows_dev, cols_dev = grads.shape
    groups = lax.axis_size("fsdp")
    planes = groups // 2
    rows = rows_dev * groups
    cols = cols_dev * lax.axis_size("grp")
    factor = 0.2 * math.sqrt(max(rows, cols))
    at = lax.axis_index("grp")
    me = lax.axis_index("fsdp")
    along = jnp.stack([lax.rem(at, SIDE), lax.div(at, SIDE)]).astype(jnp.int32)
    place = jnp.where(lax.rem(me, 2) == 0, along, along[::-1])
    spot = jnp.stack([lax.div(me, 2), lax.rem(me, 2)]).astype(jnp.int32)
    table, *sends = plan(owner, spot, grads)
    own, give = sort(over_planes(sends, 1))
    got = swap(give)
    own, got = own.reshape(rows // 2, cols_dev), got.reshape(rows // 2, cols_dev)
    parts = gram_quarter(place, gather(own, got, 0))
    parts = add(gather(*parts, 1))
    done = step(place, own, got, gather(*parts, 0), factor, planes)
    back = over_planes(done, -1)
    mine, give, rest = pick(table, spot, back)
    sends = merge(table, spot, mine, swap(give))
    came = over_planes(sends, 1)
    update = update_of(table, spot, back, swap(rest))
    owned = second_slot(spot, came, first_slot(table, spot, done))
    return (update, owned)


def solution(mesh):
    return jax.shard_map(
        on_device,
        mesh=mesh,
        in_specs=(P(None, "fsdp", "grp"), P()),
        out_specs=(P(None, "fsdp", "grp"), P("fsdp", None, "grp")),
        check_vma=False,
    )
```

```python
import functools
import math

import jax
import jax.numpy as jnp
from jax import lax
from jax.experimental import pallas as pl
from jax.experimental.pallas import tpu as pltpu
from jax.sharding import PartitionSpec as P

MOST = 2
SIDE = 4
BLOCK = 256
PIECE = BLOCK // SIDE
MIB = 1024 * 1024

VMEM = pl.BlockSpec(memory_space=pltpu.VMEM)
SMEM = pl.BlockSpec(memory_space=pltpu.SMEM)
ANY = pl.BlockSpec(memory_space=pl.ANY)


def params(mib):
    return pltpu.CompilerParams(vmem_limit_bytes=mib * MIB)


def shape_of(*dims, dtype=jnp.bfloat16):
    return jax.ShapeDtypeStruct(dims, dtype)


def cost(flops, size):
    return pl.CostEstimate(flops=flops, bytes_accessed=size, transcendentals=0)


def part(at, size):
    return pl.ds(pl.multiple_of(lax.rem(at, SIDE) * size, size), size)


def pairs_of(rows):
    side = rows // BLOCK
    return [(i, j) for i in range(side) for j in range(i + 1)]


def move_all(moves, sems):
    copies = [pltpu.make_async_copy(a, b, sems.at[k]) for k, (a, b) in enumerate(moves)]
    for copy in copies:
        copy.start()
    for copy in copies:
        copy.wait()


def group_at(spot_ref, away, other, planes):
    core = spot_ref[1]
    return 2 * lax.rem(spot_ref[0] + away, planes) + (1 - core if other else core)


def plan_kernel(owner_ref, spot_ref, grads_ref, table_ref, *refs):
    outs, (empty_ref, held, sem) = refs[:-3], refs[-3:]
    count, planes = owner_ref.shape[0], len(outs)
    copy = pltpu.make_async_copy(grads_ref, held, sem)
    copy.start()
    for g in range(count):
        table_ref[1, g] = 0
        table_ref[2, g] = -1
        table_ref[3, g] = -1
    for e in range(count):
        g = owner_ref[e]
        seen = table_ref[1, g]
        table_ref[1, g] = seen + 1
        table_ref[jnp.where(seen == 0, 0, 2), g] = e
    n = jnp.int32(0)
    for g in range(count):
        empty_ref[n] = g
        n = n + (table_ref[1, g] == 0).astype(jnp.int32)
    n = jnp.int32(0)
    for g in range(count):
        e = table_ref[2, g]
        two = e >= 0
        h = jnp.where(two, empty_ref[n], count)
        table_ref[2, g] = jnp.where(two, h, -1)
        table_ref[0, h] = e
        table_ref[3, h] = g
        n = n + two.astype(jnp.int32)
    copy.wait()
    for away in range(planes):
        for other in range(2):
            outs[away][other] = held[table_ref[0, group_at(spot_ref, away, other, planes)]]


def plan(owner, spot, grads):
    count, rows, cols = grads.shape
    planes = count // 2
    return pl.pallas_call(
        plan_kernel,
        out_shape=(shape_of(4, count + 1, dtype=jnp.int32),)
        + (shape_of(2, rows, cols),) * planes,
        in_specs=[SMEM, SMEM, ANY],
        out_specs=(SMEM,) + (VMEM,) * planes,
        scratch_shapes=[
            pltpu.SMEM((count + 1,), jnp.int32),
            pltpu.VMEM(grads.shape, grads.dtype),
            pltpu.SemaphoreType.DMA,
        ],
        compiler_params=params(8),
        name="plan",
    )(owner, spot, grads)


def sort_kernel(*refs):
    ins, (own_ref, give_ref) = in_place(refs[:-2]), refs[-2:]
    for k, ref in enumerate(ins):
        own_ref[k] = ref[0]
        give_ref[k] = ref[1]


def sort(blocks):
    planes = len(blocks)
    _, rows, cols = blocks[0].shape
    return pl.pallas_call(
        sort_kernel,
        out_shape=(shape_of(planes, rows, cols),) * 2,
        in_specs=[VMEM] * planes,
        out_specs=(VMEM,) * 2,
        compiler_params=params(8),
        name="sort",
    )(*in_turn(blocks))


def split(number, shape):
    rest = jnp.broadcast_to(number, shape)
    row = lax.broadcasted_iota(jnp.int32, shape, 0)
    parts = jnp.zeros(shape, jnp.float32)
    for k in range(3):
        top = lax.reduce_precision(rest, 8, 7)
        parts = jnp.where(row == k, top, parts)
        rest = rest - top
    return parts.astype(jnp.bfloat16)


def gram_sums(place_ref, own, got, acc, picked, write):
    each = own[0].shape[0] // BLOCK
    side = 2 * each
    turn = lax.rem(place_ref[0], SIDE) * PIECE
    lists = (own, got)

    def block(s, i):
        start = (i % each) * BLOCK
        return lists[i // each][s][start : start + BLOCK, :]

    for s in range(len(own)):
        for i in range(side):
            start = pl.multiple_of((i % each) * BLOCK + turn, PIECE)
            picked[s, i * PIECE : (i + 1) * PIECE, :] = lists[i // each][s][pl.ds(start, PIECE), :]
    index = {pair: t for t, pair in enumerate(pairs_of(side * BLOCK))}
    for j in range(side):
        total = jnp.zeros(((side - j) * PIECE, BLOCK), jnp.float32)
        for s in range(len(own)):
            total = total + lax.dot_general(
                picked[s, j * PIECE :, :],
                block(s, j),
                (((1,), (1,)), ((), ())),
                preferred_element_type=jnp.float32,
            )
        for i in range(j, side):
            t = index[i, j]
            value = total[(i - j) * PIECE : (i - j + 1) * PIECE, :]
            write(t, value if acc is None else value + acc[t])
    total = jnp.zeros((1, BLOCK), jnp.float32)
    for s in range(len(own)):
        for i in range(side):
            values = block(s, i).astype(jnp.float32)
            total = total + jnp.sum(values * values, axis=0, keepdims=True)
    return jnp.sum(total, axis=1, keepdims=True)


def gram_first_kernel(place_ref, *refs):
    own, got, (acc, square, picked) = refs[:6:2], (refs[1], refs[5], refs[3]), refs[6:]

    def write(t, value):
        acc[t] = value

    total = gram_sums(place_ref, own, got, None, picked, write)
    square[...] = jnp.broadcast_to(total, square.shape)


def gram_last_kernel(place_ref, own, got, acc, square, first, second, picked):
    cut = first.shape[0]

    def write(t, value):
        (first, second)[t // cut][t % cut] = value.astype(jnp.bfloat16)

    total = gram_sums(place_ref, [own], [got], acc, picked, write)
    second[second.shape[0] - 1] = split(total + square[0:1, :], (PIECE, BLOCK))


def gram_quarter(place, lists):
    own, got = lists
    rows = 2 * own[0].shape[0]
    blocks = len(pairs_of(rows))
    cut = (blocks + 1) // 2
    acc, square = pl.pallas_call(
        gram_first_kernel,
        out_shape=(
            shape_of(blocks, PIECE, BLOCK, dtype=jnp.float32),
            shape_of(8, BLOCK, dtype=jnp.float32),
        ),
        in_specs=[SMEM] + [VMEM] * 6,
        out_specs=(VMEM,) * 2,
        scratch_shapes=[pltpu.VMEM((SIDE - 1, rows // SIDE, BLOCK), jnp.bfloat16)],
        compiler_params=params(16),
        cost_estimate=cost(3 * blocks * BLOCK**3 // 2, 4 * MIB),
        name="gram_first",
    )(place, own[0], got[0], own[1], got[3], own[3], got[1])
    return pl.pallas_call(
        gram_last_kernel,
        out_shape=(shape_of(cut, PIECE, BLOCK), shape_of(blocks + 1 - cut, PIECE, BLOCK)),
        in_specs=[SMEM] + [VMEM] * 4,
        out_specs=(VMEM,) * 2,
        scratch_shapes=[pltpu.VMEM((1, rows // SIDE, BLOCK), jnp.bfloat16)],
        compiler_params=params(16),
        name="gram_last",
    )(place, own[2], got[2], acc, square)


def add_kernel(rows, *refs):
    lists, (first, second, inverse_ref) = in_lists(refs[: 2 * SIDE]), refs[2 * SIDE :]
    number = jnp.zeros((1, BLOCK), jnp.float32)
    for piece in lists[1]:
        last = piece.shape[0] - 1
        number = number + jnp.sum(piece[last].astype(jnp.float32), axis=0, keepdims=True)
    inverse = 1.0 / jnp.sqrt(number / rows + 1e-06)
    scale = inverse * inverse
    inverse_ref[...] = jnp.broadcast_to(inverse, inverse_ref.shape)
    for ins, out in zip(lists, (first, second)):
        total = ins[0][...].astype(jnp.float32)
        for other in ins[1:]:
            total = total + other[...].astype(jnp.float32)
        out[...] = jnp.where(scale > 0, total * scale, 0.0).astype(jnp.bfloat16)


def add(lists, rows):
    return pl.pallas_call(
        functools.partial(add_kernel, rows),
        out_shape=(
            shape_of(*lists[0][0].shape),
            shape_of(*lists[1][0].shape),
            shape_of(8, BLOCK, dtype=jnp.float32),
        ),
        in_specs=[VMEM] * (2 * SIDE),
        out_specs=(VMEM,) * 3,
        compiler_params=params(12),
        name="add",
    )(*out_of_lists(lists))


def step_kernel(pairs, factor, planes, place_ref, own_ref, got_ref, inverse_ref, *refs):
    early, late = in_lists(refs[: 2 * SIDE])
    outs, (gram, normed, left) = refs[2 * SIDE : -3], refs[-3:]
    half = own_ref.shape[0]
    blocks = early[0].shape[0]
    side = 2 * half // BLOCK
    for k, ref in enumerate((own_ref, got_ref)):
        for i in range(half // BLOCK):
            values = ref[i * BLOCK : (i + 1) * BLOCK, :].astype(jnp.float32)
            normed[k * half + i * BLOCK : k * half + (i + 1) * BLOCK, :] = (
                values * inverse_ref[0:1, :]
            ).astype(jnp.bfloat16)
    for t, (i, j) in enumerate(pairs):
        source, u = (early, t) if t < blocks else (late, t - blocks)
        for s in range(SIDE):
            p = lax.rem(place_ref[0] - s + SIDE, SIDE)
            rows = pl.ds(pl.multiple_of(i * BLOCK + p * PIECE, PIECE), PIECE)
            gram[rows, j * BLOCK : (j + 1) * BLOCK] = source[s][u]
    for i, j in pairs:
        if i != j:
            block = gram[i * BLOCK : (i + 1) * BLOCK, j * BLOCK : (j + 1) * BLOCK]
            gram[j * BLOCK : (j + 1) * BLOCK, i * BLOCK : (i + 1) * BLOCK] = block.T
    for i in range(side):
        rows = slice(i * BLOCK, (i + 1) * BLOCK)
        left[rows, :] = jnp.dot(
            gram[rows, :], normed[...], preferred_element_type=jnp.float32
        ).astype(jnp.bfloat16)
    each = half // planes
    for k in range(2):
        for away in range(0, planes, 2):
            rows = slice(k * half + away * each, k * half + (away + 2) * each)
            right = jnp.dot(gram[rows, :], left[...], preferred_element_type=jnp.float32)
            mixed = (
                3.4445 * normed[rows, :].astype(jnp.float32)
                - 4.775 * left[rows, :].astype(jnp.float32)
                + 2.0315 * right
            )
            values = (factor * mixed).astype(jnp.bfloat16)
            outs[away][k] = values[:each]
            outs[away + 1][k] = values[each:]


def step(place, own, got, inverse, lists, factor, planes):
    half, cols = own.shape
    rows = 2 * half
    return pl.pallas_call(
        functools.partial(step_kernel, pairs_of(rows), factor, planes),
        out_shape=(shape_of(2, half // planes, cols),) * planes,
        in_specs=[SMEM] + [VMEM] * (3 + 2 * SIDE),
        out_specs=(VMEM,) * planes,
        scratch_shapes=[
            pltpu.VMEM((rows, rows), jnp.bfloat16),
            pltpu.VMEM((rows, cols), jnp.bfloat16),
            pltpu.VMEM((rows, cols), jnp.bfloat16),
        ],
        compiler_params=params(28),
        cost_estimate=cost(4 * rows * rows * cols, 6 * 1024 * 1024),
        name="step",
    )(place, own, got, inverse, *out_of_lists(lists))


def pick_kernel(planes, table_ref, spot_ref, *refs):
    ins, (mine_ref, give_ref, rest_ref) = in_place(refs[:planes]), refs[planes:]
    for up, ref in enumerate(ins):
        owner = table_ref[3, group_at(spot_ref, up, 0, planes)]
        away = lax.rem(lax.div(jnp.maximum(owner, 0), 2) - spot_ref[0] + planes, planes)
        here = lax.rem(jnp.maximum(owner, 0), 2) == spot_ref[1]

        @pl.when(jnp.logical_and(owner >= 0, here))
        def _():
            mine_ref[away] = ref[...]

        @pl.when(jnp.logical_and(owner >= 0, jnp.logical_not(here)))
        def _():
            give_ref[away] = ref[...]

        rest_ref[up] = ref[1]


def pick(table, spot, back):
    planes = len(back)
    block = back[0].shape
    return pl.pallas_call(
        functools.partial(pick_kernel, planes),
        out_shape=(shape_of(planes, *block),) * 2 + (shape_of(planes, *block[1:]),),
        in_specs=[SMEM] * 2 + [VMEM] * planes,
        out_specs=(VMEM,) * 3,
        compiler_params=params(8),
        name="pick",
    )(table, spot, *in_turn(back))


def merge_kernel(planes, table_ref, spot_ref, mine_ref, got_ref, *outs):
    for away, out in enumerate(outs):
        helper = table_ref[2, group_at(spot_ref, away, 0, planes)]
        here = lax.rem(jnp.maximum(helper, 0), 2) == spot_ref[1]

        @pl.when(helper < 0)
        def _():
            out[...] = jnp.zeros(out.shape, out.dtype)

        @pl.when(jnp.logical_and(helper >= 0, here))
        def _():
            out[...] = mine_ref[away]

        @pl.when(jnp.logical_and(helper >= 0, jnp.logical_not(here)))
        def _():
            out[0] = got_ref[away, 1]
            out[1] = got_ref[away, 0]


def merge(table, spot, mine, got):
    planes = mine.shape[0]
    return pl.pallas_call(
        functools.partial(merge_kernel, planes),
        out_shape=(shape_of(*mine.shape[1:]),) * planes,
        in_specs=[SMEM] * 2 + [VMEM] * 2,
        out_specs=(VMEM,) * planes,
        compiler_params=params(8),
        name="merge",
    )(table, spot, mine, got)


def update_kernel(planes, table_ref, spot_ref, *refs):
    ins, (rest_ref, out_ref, sems) = in_place(refs[:planes]), refs[planes:]
    moves = []
    for away in range(planes):
        e = table_ref[0, group_at(spot_ref, away, 0, planes)]
        moves.append((ins[away].at[0], out_ref.at[e]))
        e = table_ref[0, group_at(spot_ref, away, 1, planes)]
        moves.append((rest_ref.at[away], out_ref.at[e]))
    move_all(moves, sems)


def update_of(table, spot, back, rest):
    planes, rows, cols = rest.shape
    return pl.pallas_call(
        functools.partial(update_kernel, planes),
        out_shape=shape_of(2 * planes, rows, cols),
        in_specs=[SMEM] * 2 + [VMEM] * (planes + 1),
        out_specs=ANY,
        scratch_shapes=[pltpu.SemaphoreType.DMA((2 * planes,))],
        compiler_params=params(8),
        name="update",
    )(table, spot, *in_turn(back), rest)


def slot_moves(spot_ref, ins, out_ref, slot):
    planes = len(ins)
    moves = []
    for away, ref in enumerate(ins):
        for k in range(2):
            rows = ref.shape[1]
            start = group_at(spot_ref, planes - away, k, planes) * rows
            to = out_ref.at[slot, pl.ds(pl.multiple_of(start, rows), rows)]
            moves.append((ref.at[k], to))
    return moves


def first_kernel(planes, table_ref, spot_ref, *refs):
    ins, (out_ref, zero, sems) = refs[:planes], refs[planes:]
    moves = slot_moves(spot_ref, ins, out_ref, 0)
    owns = table_ref[1, group_at(spot_ref, 0, 0, planes)] > 0

    @pl.when(owns)
    def _():
        move_all(moves, sems)

    @pl.when(jnp.logical_not(owns))
    def _():
        zero[...] = jnp.zeros(zero.shape, zero.dtype)
        move_all([(zero, b) for _, b in moves], sems)


def second_kernel(planes, spot_ref, *refs):
    ins, (_, out_ref, sems) = in_place(refs[:planes]), refs[planes:]
    move_all(slot_moves(spot_ref, ins, out_ref, 1), sems)


def first_slot(table, spot, done):
    planes = len(done)
    _, rows, cols = done[0].shape
    return pl.pallas_call(
        functools.partial(first_kernel, planes),
        out_shape=shape_of(MOST, 2 * planes * rows, cols),
        in_specs=[SMEM] * 2 + [VMEM] * planes,
        out_specs=ANY,
        scratch_shapes=[
            pltpu.VMEM((rows, cols), jnp.bfloat16),
            pltpu.SemaphoreType.DMA((2 * planes,)),
        ],
        compiler_params=params(8),
        name="first_slot",
    )(table, spot, *done)


def second_slot(spot, came, owned):
    planes = len(came)
    return pl.pallas_call(
        functools.partial(second_kernel, planes),
        out_shape=shape_of(*owned.shape),
        in_specs=[SMEM] + [VMEM] * planes + [ANY],
        out_specs=ANY,
        scratch_shapes=[pltpu.SemaphoreType.DMA((2 * planes,))],
        input_output_aliases={planes + 1: 0},
        compiler_params=params(8),
        name="second_slot",
    )(spot, *in_turn(came), owned)


def neighbour(value, order, amount):
    groups, places = lax.axis_size("fsdp"), SIDE * SIDE
    moves = []
    for at in range(groups * places):
        group, place = divmod(at, places)
        y, x = divmod(place, SIDE)
        if group % 2 == order:
            x = (x + amount) % SIDE
        else:
            y = (y + amount) % SIDE
        moves.append((at, group * places + y * SIDE + x))
    return lax.ppermute(value, ("fsdp", "grp"), moves)


def gather(first, second, order):
    one = [first, neighbour(first, order, 1), None, neighbour(first, order, -1)]
    two = [second, neighbour(second, order, 1), None, neighbour(second, order, -1)]
    one[2] = neighbour(one[1], order, 1)
    two[2] = neighbour(two[3], order, -1)
    return one, two


TRAVEL = ((0, 0), (1, 0), (0, 1), (1, 3), (0, 3), (1, 1), (0, 2), (1, 2))


def out_of_lists(lists):
    return [lists[k][s] for k, s in TRAVEL]


def in_lists(refs):
    return [[refs[TRAVEL.index((k, s))] for s in range(SIDE)] for k in range(2)]


def over_planes(blocks, sign):
    planes = len(blocks)
    got = list(blocks)
    for away in farthest_first(planes)[1:]:
        moves = []
        for group in range(2 * planes):
            plane, core = divmod(group, 2)
            moves.append((group, 2 * ((plane + sign * away) % planes) + core))
        got[away] = lax.ppermute(blocks[away], "fsdp", moves)
    return got


def farthest_first(planes):
    return sorted(range(planes), key=lambda a: -min(a, planes - a) if a else -planes)


def in_turn(blocks):
    return [blocks[away] for away in farthest_first(len(blocks))]


def in_place(refs):
    order = farthest_first(len(refs))
    return [refs[order.index(away)] for away in range(len(refs))]


def swap(value):
    groups = lax.axis_size("fsdp")
    return lax.ppermute(value, "fsdp", [(g, g ^ 1) for g in range(groups)])


def on_device(grads, owner):
    count, rows_dev, cols_dev = grads.shape
    groups = lax.axis_size("fsdp")
    planes = groups // 2
    rows = rows_dev * groups
    cols = cols_dev * lax.axis_size("grp")
    factor = 0.2 * math.sqrt(max(rows, cols))
    at = lax.axis_index("grp")
    me = lax.axis_index("fsdp")
    along = jnp.stack([lax.rem(at, SIDE), lax.div(at, SIDE)]).astype(jnp.int32)
    place = jnp.where(lax.rem(me, 2) == 0, along, along[::-1])
    spot = jnp.stack([lax.div(me, 2), lax.rem(me, 2)]).astype(jnp.int32)
    table, *sends = plan(owner, spot, grads)
    own, give = sort(over_planes(sends, 1))
    got = swap(give)
    own, got = own.reshape(rows // 2, cols_dev), got.reshape(rows // 2, cols_dev)
    parts = gram_quarter(place, gather(own, got, 0))
    *parts, inverse = add(gather(*parts, 1), rows)
    done = step(place, own, got, inverse, gather(*parts, 0), factor, planes)
    back = over_planes(done, -1)
    mine, give, rest = pick(table, spot, back)
    sends = merge(table, spot, mine, swap(give))
    came = over_planes(sends, 1)
    update = update_of(table, spot, back, swap(rest))
    owned = second_slot(spot, came, first_slot(table, spot, done))
    return (update, owned)


def solution(mesh):
    return jax.shard_map(
        on_device,
        mesh=mesh,
        in_specs=(P(None, "fsdp", "grp"), P()),
        out_specs=(P(None, "fsdp", "grp"), P("fsdp", None, "grp")),
        check_vma=False,
    )
```

```python
import functools
import math

import jax
import jax.numpy as jnp
from jax import lax
from jax.experimental import pallas as pl
from jax.experimental.pallas import tpu as pltpu
from jax.sharding import PartitionSpec as P

MOST = 2
SIDE = 4
BLOCK = 256
PIECE = BLOCK // SIDE
MIB = 1024 * 1024

VMEM = pl.BlockSpec(memory_space=pltpu.VMEM)
SMEM = pl.BlockSpec(memory_space=pltpu.SMEM)
ANY = pl.BlockSpec(memory_space=pl.ANY)


def params(mib):
    return pltpu.CompilerParams(vmem_limit_bytes=mib * MIB)


def shape_of(*dims, dtype=jnp.bfloat16):
    return jax.ShapeDtypeStruct(dims, dtype)


def cost(flops, size):
    return pl.CostEstimate(flops=flops, bytes_accessed=size, transcendentals=0)


def spot_here():
    me = lax.axis_index("fsdp")
    return lax.div(me, 2), lax.rem(me, 2)


def place_here():
    at = lax.axis_index("grp")
    x, y = lax.rem(at, SIDE), lax.div(at, SIDE)
    _, core = spot_here()
    return jnp.where(core == 0, x, y), jnp.where(core == 0, y, x)


def pairs_of(rows):
    side = rows // BLOCK
    return [(i, j) for i in range(side) for j in range(i + 1)]


def move_all(moves, sems):
    copies = [pltpu.make_async_copy(a, b, sems.at[k]) for k, (a, b) in enumerate(moves)]
    for copy in copies:
        copy.start()
    for copy in copies:
        copy.wait()


def group_at(away, other, planes):
    plane, core = spot_here()
    return 2 * lax.rem(plane + away, planes) + (1 - core if other else core)


def plan_kernel(owner_ref, grads_ref, table_ref, *refs):
    outs, (empty_ref, held, sem) = refs[:-3], refs[-3:]
    count, planes = owner_ref.shape[0], len(outs)
    copy = pltpu.make_async_copy(grads_ref, held, sem)
    copy.start()
    for g in range(count):
        table_ref[1, g] = 0
        table_ref[2, g] = -1
        table_ref[3, g] = -1
    for e in range(count):
        g = owner_ref[e]
        seen = table_ref[1, g]
        table_ref[1, g] = seen + 1
        table_ref[jnp.where(seen == 0, 0, 2), g] = e
    n = jnp.int32(0)
    for g in range(count):
        empty_ref[n] = g
        n = n + (table_ref[1, g] == 0).astype(jnp.int32)
    n = jnp.int32(0)
    for g in range(count):
        e = table_ref[2, g]
        two = e >= 0
        h = jnp.where(two, empty_ref[n], count)
        table_ref[2, g] = jnp.where(two, h, -1)
        table_ref[0, h] = e
        table_ref[3, h] = g
        n = n + two.astype(jnp.int32)
    copy.wait()
    for away in range(planes):
        for other in range(2):
            outs[away][other] = held[table_ref[0, group_at(away, other, planes)]]


def plan(owner, grads):
    count, rows, cols = grads.shape
    planes = count // 2
    return pl.pallas_call(
        plan_kernel,
        out_shape=(shape_of(4, count + 1, dtype=jnp.int32),)
        + (shape_of(2, rows, cols),) * planes,
        in_specs=[SMEM, ANY],
        out_specs=(SMEM,) + (VMEM,) * planes,
        scratch_shapes=[
            pltpu.SMEM((count + 1,), jnp.int32),
            pltpu.VMEM(grads.shape, grads.dtype),
            pltpu.SemaphoreType.DMA,
        ],
        compiler_params=params(8),
        name="plan",
    )(owner, grads)


def sort_kernel(*refs):
    ins, (own_ref, give_ref) = in_place(refs[:-2]), refs[-2:]
    for k, ref in enumerate(ins):
        own_ref[k] = ref[0]
        give_ref[k] = ref[1]


def sort(blocks):
    planes = len(blocks)
    _, rows, cols = blocks[0].shape
    return pl.pallas_call(
        sort_kernel,
        out_shape=(shape_of(planes, rows, cols),) * 2,
        in_specs=[VMEM] * planes,
        out_specs=(VMEM,) * 2,
        compiler_params=params(8),
        name="sort",
    )(*in_turn(blocks))


def split(number, shape):
    rest = jnp.broadcast_to(number, shape)
    row = lax.broadcasted_iota(jnp.int32, shape, 0)
    parts = jnp.zeros(shape, jnp.float32)
    for k in range(3):
        top = lax.reduce_precision(rest, 8, 7)
        parts = jnp.where(row == k, top, parts)
        rest = rest - top
    return parts.astype(jnp.bfloat16)


def gram_sums(own, got, acc, picked, write):
    each = own[0].shape[0] // BLOCK
    side = 2 * each
    turn = place_here()[0] * PIECE
    lists = (own, got)

    def block(s, i):
        start = (i % each) * BLOCK
        return lists[i // each][s][start : start + BLOCK, :]

    for s in range(len(own)):
        for i in range(side):
            start = pl.multiple_of((i % each) * BLOCK + turn, PIECE)
            picked[s, i * PIECE : (i + 1) * PIECE, :] = lists[i // each][s][pl.ds(start, PIECE), :]
    index = {pair: t for t, pair in enumerate(pairs_of(side * BLOCK))}
    for j in range(side):
        total = jnp.zeros(((side - j) * PIECE, BLOCK), jnp.float32)
        for s in range(len(own)):
            total = total + lax.dot_general(
                picked[s, j * PIECE :, :],
                block(s, j),
                (((1,), (1,)), ((), ())),
                preferred_element_type=jnp.float32,
            )
        for i in range(j, side):
            t = index[i, j]
            value = total[(i - j) * PIECE : (i - j + 1) * PIECE, :]
            write(t, value if acc is None else value + acc[t])
    total = jnp.zeros((1, BLOCK), jnp.float32)
    for s in range(len(own)):
        for i in range(side):
            values = block(s, i).astype(jnp.float32)
            total = total + jnp.sum(values * values, axis=0, keepdims=True)
    return jnp.sum(total, axis=1, keepdims=True)


def gram_first_kernel(*refs):
    own, got, (acc, square, picked) = refs[:6:2], (refs[1], refs[5], refs[3]), refs[6:]

    def write(t, value):
        acc[t] = value

    total = gram_sums(own, got, None, picked, write)
    square[...] = jnp.broadcast_to(total, square.shape)


def gram_last_kernel(own, got, acc, square, first, second, picked):
    cut = first.shape[0]

    def write(t, value):
        (first, second)[t // cut][t % cut] = value.astype(jnp.bfloat16)

    total = gram_sums([own], [got], acc, picked, write)
    second[second.shape[0] - 1] = split(total + square[0:1, :], (PIECE, BLOCK))


def gram_quarter(lists):
    own, got = lists
    rows = 2 * own[0].shape[0]
    blocks = len(pairs_of(rows))
    cut = (blocks + 1) // 2
    acc, square = pl.pallas_call(
        gram_first_kernel,
        out_shape=(
            shape_of(blocks, PIECE, BLOCK, dtype=jnp.float32),
            shape_of(8, BLOCK, dtype=jnp.float32),
        ),
        in_specs=[VMEM] * 6,
        out_specs=(VMEM,) * 2,
        scratch_shapes=[pltpu.VMEM((SIDE - 1, rows // SIDE, BLOCK), jnp.bfloat16)],
        compiler_params=params(16),
        cost_estimate=cost(3 * blocks * BLOCK**3 // 2, 4 * MIB),
        name="gram_first",
    )(own[0], got[0], own[1], got[3], own[3], got[1])
    return pl.pallas_call(
        gram_last_kernel,
        out_shape=(shape_of(cut, PIECE, BLOCK), shape_of(blocks + 1 - cut, PIECE, BLOCK)),
        in_specs=[VMEM] * 4,
        out_specs=(VMEM,) * 2,
        scratch_shapes=[pltpu.VMEM((1, rows // SIDE, BLOCK), jnp.bfloat16)],
        compiler_params=params(16),
        name="gram_last",
    )(own[2], got[2], acc, square)


def add_kernel(rows, *refs):
    lists, (first, second, inverse_ref) = in_lists(refs[: 2 * SIDE]), refs[2 * SIDE :]
    number = jnp.zeros((1, BLOCK), jnp.float32)
    for piece in lists[1]:
        last = piece.shape[0] - 1
        number = number + jnp.sum(piece[last].astype(jnp.float32), axis=0, keepdims=True)
    inverse = 1.0 / jnp.sqrt(number / rows + 1e-06)
    scale = inverse * inverse
    inverse_ref[...] = jnp.broadcast_to(inverse, inverse_ref.shape)
    for ins, out in zip(lists, (first, second)):
        total = ins[0][...].astype(jnp.float32)
        for other in ins[1:]:
            total = total + other[...].astype(jnp.float32)
        out[...] = jnp.where(scale > 0, total * scale, 0.0).astype(jnp.bfloat16)


def add(lists, rows):
    return pl.pallas_call(
        functools.partial(add_kernel, rows),
        out_shape=(
            shape_of(*lists[0][0].shape),
            shape_of(*lists[1][0].shape),
            shape_of(8, BLOCK, dtype=jnp.float32),
        ),
        in_specs=[VMEM] * (2 * SIDE),
        out_specs=(VMEM,) * 3,
        compiler_params=params(12),
        name="add",
    )(*out_of_lists(lists))


def step_kernel(pairs, factor, planes, own_ref, got_ref, inverse_ref, *refs):
    early, late = in_lists(refs[: 2 * SIDE])
    outs, (gram, normed, left) = refs[2 * SIDE : -3], refs[-3:]
    half = own_ref.shape[0]
    blocks = early[0].shape[0]
    side = 2 * half // BLOCK
    first, _ = place_here()
    for k, ref in enumerate((own_ref, got_ref)):
        for i in range(half // BLOCK):
            values = ref[i * BLOCK : (i + 1) * BLOCK, :].astype(jnp.float32)
            normed[k * half + i * BLOCK : k * half + (i + 1) * BLOCK, :] = (
                values * inverse_ref[0:1, :]
            ).astype(jnp.bfloat16)
    for t, (i, j) in enumerate(pairs):
        source, u = (early, t) if t < blocks else (late, t - blocks)
        for s in range(SIDE):
            p = lax.rem(first - s + SIDE, SIDE)
            rows = pl.ds(pl.multiple_of(i * BLOCK + p * PIECE, PIECE), PIECE)
            gram[rows, j * BLOCK : (j + 1) * BLOCK] = source[s][u]
    for i, j in pairs:
        if i != j:
            block = gram[i * BLOCK : (i + 1) * BLOCK, j * BLOCK : (j + 1) * BLOCK]
            gram[j * BLOCK : (j + 1) * BLOCK, i * BLOCK : (i + 1) * BLOCK] = block.T
    for i in range(side):
        rows = slice(i * BLOCK, (i + 1) * BLOCK)
        left[rows, :] = jnp.dot(
            gram[rows, :], normed[...], preferred_element_type=jnp.float32
        ).astype(jnp.bfloat16)
    each = half // planes
    for k in range(2):
        for away in range(0, planes, 2):
            rows = slice(k * half + away * each, k * half + (away + 2) * each)
            right = jnp.dot(gram[rows, :], left[...], preferred_element_type=jnp.float32)
            mixed = (
                3.4445 * normed[rows, :].astype(jnp.float32)
                - 4.775 * left[rows, :].astype(jnp.float32)
                + 2.0315 * right
            )
            values = (factor * mixed).astype(jnp.bfloat16)
            outs[away][k] = values[:each]
            outs[away + 1][k] = values[each:]


def step(own, got, inverse, lists, factor, planes):
    half, cols = own.shape
    rows = 2 * half
    return pl.pallas_call(
        functools.partial(step_kernel, pairs_of(rows), factor, planes),
        out_shape=(shape_of(2, half // planes, cols),) * planes,
        in_specs=[VMEM] * (3 + 2 * SIDE),
        out_specs=(VMEM,) * planes,
        scratch_shapes=[
            pltpu.VMEM((rows, rows), jnp.bfloat16),
            pltpu.VMEM((rows, cols), jnp.bfloat16),
            pltpu.VMEM((rows, cols), jnp.bfloat16),
        ],
        compiler_params=params(28),
        cost_estimate=cost(4 * rows * rows * cols, 6 * 1024 * 1024),
        name="step",
    )(own, got, inverse, *out_of_lists(lists))


def pick_kernel(planes, table_ref, *refs):
    ins, (mine_ref, give_ref) = in_place(refs[:planes]), refs[planes:]
    for up, ref in enumerate(ins):
        owner = table_ref[3, group_at(up, 0, planes)]
        away = lax.rem(lax.div(jnp.maximum(owner, 0), 2) - spot_here()[0] + planes, planes)
        here = lax.rem(jnp.maximum(owner, 0), 2) == spot_here()[1]

        @pl.when(jnp.logical_and(owner >= 0, here))
        def _():
            mine_ref[away] = ref[...]

        @pl.when(jnp.logical_and(owner >= 0, jnp.logical_not(here)))
        def _():
            give_ref[away] = ref[...]


def pick(table, back):
    planes = len(back)
    block = back[0].shape
    return pl.pallas_call(
        functools.partial(pick_kernel, planes),
        out_shape=(shape_of(planes, *block),) * 2,
        in_specs=[SMEM] + [VMEM] * planes,
        out_specs=(VMEM,) * 2,
        compiler_params=params(8),
        name="pick",
    )(table, *in_turn(back))


def merge_kernel(planes, table_ref, mine_ref, got_ref, *outs):
    for away, out in enumerate(outs):
        helper = table_ref[2, group_at(away, 0, planes)]
        here = lax.rem(jnp.maximum(helper, 0), 2) == spot_here()[1]

        @pl.when(helper < 0)
        def _():
            out[...] = jnp.zeros(out.shape, out.dtype)

        @pl.when(jnp.logical_and(helper >= 0, here))
        def _():
            out[...] = mine_ref[away]

        @pl.when(jnp.logical_and(helper >= 0, jnp.logical_not(here)))
        def _():
            out[0] = got_ref[away, 1]
            out[1] = got_ref[away, 0]


def merge(table, mine, got):
    planes = mine.shape[0]
    return pl.pallas_call(
        functools.partial(merge_kernel, planes),
        out_shape=(shape_of(*mine.shape[1:]),) * planes,
        in_specs=[SMEM] + [VMEM] * 2,
        out_specs=(VMEM,) * planes,
        compiler_params=params(8),
        name="merge",
    )(table, mine, got)


def update_kernel(planes, table_ref, *refs):
    own_ref, rest_ref, out_ref, sems = refs
    moves = []
    for away in range(planes):
        e = table_ref[0, group_at(away, 0, planes)]
        moves.append((own_ref.at[away], out_ref.at[e]))
        e = table_ref[0, group_at(away, 1, planes)]
        moves.append((rest_ref.at[away], out_ref.at[e]))
    move_all(moves, sems)


def update_of(table, own, rest):
    planes, rows, cols = rest.shape
    return pl.pallas_call(
        functools.partial(update_kernel, planes),
        out_shape=shape_of(2 * planes, rows, cols),
        in_specs=[SMEM] + [VMEM] * 2,
        out_specs=ANY,
        scratch_shapes=[pltpu.SemaphoreType.DMA((2 * planes,))],
        compiler_params=params(8),
        name="update",
    )(table, own, rest)


def slot_moves(ins, out_ref, slot):
    planes = len(ins)
    moves = []
    for away, ref in enumerate(ins):
        for k in range(2):
            rows = ref.shape[1]
            start = group_at(planes - away, k, planes) * rows
            to = out_ref.at[slot, pl.ds(pl.multiple_of(start, rows), rows)]
            moves.append((ref.at[k], to))
    return moves


def first_kernel(planes, table_ref, *refs):
    ins, (out_ref, zero, sems) = refs[:planes], refs[planes:]
    moves = slot_moves(ins, out_ref, 0)
    owns = table_ref[1, group_at(0, 0, planes)] > 0

    @pl.when(owns)
    def _():
        move_all(moves, sems)

    @pl.when(jnp.logical_not(owns))
    def _():
        zero[...] = jnp.zeros(zero.shape, zero.dtype)
        move_all([(zero, b) for _, b in moves], sems)


def second_kernel(planes, *refs):
    ins, (_, out_ref, sems) = in_place(refs[:planes]), refs[planes:]
    move_all(slot_moves(ins, out_ref, 1), sems)


def first_slot(table, done):
    planes = len(done)
    _, rows, cols = done[0].shape
    return pl.pallas_call(
        functools.partial(first_kernel, planes),
        out_shape=shape_of(MOST, 2 * planes * rows, cols),
        in_specs=[SMEM] + [VMEM] * planes,
        out_specs=ANY,
        scratch_shapes=[
            pltpu.VMEM((rows, cols), jnp.bfloat16),
            pltpu.SemaphoreType.DMA((2 * planes,)),
        ],
        compiler_params=params(8),
        name="first_slot",
    )(table, *done)


def second_slot(came, owned):
    planes = len(came)
    return pl.pallas_call(
        functools.partial(second_kernel, planes),
        out_shape=shape_of(*owned.shape),
        in_specs=[VMEM] * planes + [ANY],
        out_specs=ANY,
        scratch_shapes=[pltpu.SemaphoreType.DMA((2 * planes,))],
        input_output_aliases={planes: 0},
        compiler_params=params(8),
        name="second_slot",
    )(*in_turn(came), owned)


def neighbour(value, order, amount):
    groups, places = lax.axis_size("fsdp"), SIDE * SIDE
    moves = []
    for at in range(groups * places):
        group, place = divmod(at, places)
        y, x = divmod(place, SIDE)
        if group % 2 == order:
            x = (x + amount) % SIDE
        else:
            y = (y + amount) % SIDE
        moves.append((at, group * places + y * SIDE + x))
    return lax.ppermute(value, ("fsdp", "grp"), moves)


def gather(first, second, order):
    one = [first, neighbour(first, order, 1), None, neighbour(first, order, -1)]
    two = [second, neighbour(second, order, 1), None, neighbour(second, order, -1)]
    one[2] = neighbour(one[1], order, 1)
    two[2] = neighbour(two[3], order, -1)
    return one, two


TRAVEL = ((0, 0), (1, 0), (0, 1), (1, 3), (0, 3), (1, 1), (0, 2), (1, 2))


def out_of_lists(lists):
    return [lists[k][s] for k, s in TRAVEL]


def in_lists(refs):
    return [[refs[TRAVEL.index((k, s))] for s in range(SIDE)] for k in range(2)]


def over_planes(blocks, sign):
    planes = len(blocks)
    got = list(blocks)
    for away in farthest_first(planes)[1:]:
        moves = []
        for group in range(2 * planes):
            plane, core = divmod(group, 2)
            moves.append((group, 2 * ((plane + sign * away) % planes) + core))
        got[away] = lax.ppermute(blocks[away], "fsdp", moves)
    return got


def farthest_first(planes):
    return sorted(range(planes), key=lambda a: -min(a, planes - a) if a else -planes)


def in_turn(blocks):
    return [blocks[away] for away in farthest_first(len(blocks))]


def in_place(refs):
    order = farthest_first(len(refs))
    return [refs[order.index(away)] for away in range(len(refs))]


def swap(value):
    groups = lax.axis_size("fsdp")
    return lax.ppermute(value, "fsdp", [(g, g ^ 1) for g in range(groups)])


def on_device(grads, owner):
    count, rows_dev, cols_dev = grads.shape
    groups = lax.axis_size("fsdp")
    planes = groups // 2
    rows = rows_dev * groups
    cols = cols_dev * lax.axis_size("grp")
    factor = 0.2 * math.sqrt(max(rows, cols))
    table, *sends = plan(owner, grads)
    own, give = sort(over_planes(sends, 1))
    got = swap(give)
    own, got = own.reshape(rows // 2, cols_dev), got.reshape(rows // 2, cols_dev)
    parts = gram_quarter(gather(own, got, 0))
    *parts, inverse = add(gather(*parts, 1), rows)
    done = step(own, got, inverse, gather(*parts, 0), factor, planes)
    back = over_planes(done, -1)
    mine, give = pick(table, back)
    sends = merge(table, mine, swap(give))
    came = over_planes(sends, 1)
    own, rest = sort(back)
    update = update_of(table, own, swap(rest))
    owned = second_slot(came, first_slot(table, done))
    return (update, owned)


def solution(mesh):
    return jax.shard_map(
        on_device,
        mesh=mesh,
        in_specs=(P(None, "fsdp", "grp"), P()),
        out_specs=(P(None, "fsdp", "grp"), P("fsdp", None, "grp")),
        check_vma=False,
    )
```

```python
import functools
import math

import jax
import jax.numpy as jnp
from jax import lax
from jax.experimental import pallas as pl
from jax.experimental.pallas import tpu as pltpu
from jax.sharding import PartitionSpec as P

MOST = 2
SIDE = 4
BLOCK = 256
PIECE = BLOCK // SIDE
MIB = 1024 * 1024

VMEM = pl.BlockSpec(memory_space=pltpu.VMEM)
SMEM = pl.BlockSpec(memory_space=pltpu.SMEM)
ANY = pl.BlockSpec(memory_space=pl.ANY)


def params(mib):
    return pltpu.CompilerParams(vmem_limit_bytes=mib * MIB)


def shape_of(*dims, dtype=jnp.bfloat16):
    return jax.ShapeDtypeStruct(dims, dtype)


def cost(flops, size):
    return pl.CostEstimate(flops=flops, bytes_accessed=size, transcendentals=0)


def spot_here():
    me = lax.axis_index("fsdp")
    return lax.div(me, 2), lax.rem(me, 2)


def place_here():
    at = lax.axis_index("grp")
    x, y = lax.rem(at, SIDE), lax.div(at, SIDE)
    _, core = spot_here()
    return jnp.where(core == 0, x, y), jnp.where(core == 0, y, x)


def pairs_of(rows):
    side = rows // BLOCK
    return [(i, j) for i in range(side) for j in range(i + 1)]


def move_all(moves, sems):
    copies = [pltpu.make_async_copy(a, b, sems.at[k]) for k, (a, b) in enumerate(moves)]
    for copy in copies:
        copy.start()
    for copy in copies:
        copy.wait()


def group_at(away, other, planes):
    plane, core = spot_here()
    return 2 * lax.rem(plane + away, planes) + (1 - core if other else core)


def plan_kernel(owner_ref, grads_ref, table_ref, marks_ref, *refs):
    outs, (empty_ref, held, sem) = refs[:-3], refs[-3:]
    count, planes = owner_ref.shape[0], len(outs)
    copy = pltpu.make_async_copy(grads_ref, held, sem)
    copy.start()
    for g in range(count):
        table_ref[1, g] = 0
        table_ref[2, g] = -1
        table_ref[3, g] = -1
    for e in range(count):
        g = owner_ref[e]
        seen = table_ref[1, g]
        table_ref[1, g] = seen + 1
        table_ref[jnp.where(seen == 0, 0, 2), g] = e
    n = jnp.int32(0)
    for g in range(count):
        empty_ref[n] = g
        n = n + (table_ref[1, g] == 0).astype(jnp.int32)
    n = jnp.int32(0)
    for g in range(count):
        e = table_ref[2, g]
        two = e >= 0
        h = jnp.where(two, empty_ref[n], count)
        table_ref[2, g] = jnp.where(two, h, -1)
        table_ref[0, h] = e
        table_ref[3, h] = g
        n = n + two.astype(jnp.int32)
    plane, core = spot_here()
    for away in range(planes):
        group = group_at(away, 0, planes)
        helper = table_ref[2, group]
        here = jnp.where(lax.rem(jnp.maximum(helper, 0), 2) == core, 0, 1)
        mark = jnp.where(helper < 0, -1, here)
        marks_ref[away : away + 1, :] = jnp.full((1, marks_ref.shape[1]), mark, jnp.int32)
        owner = table_ref[3, group]
        there = jnp.maximum(owner, 0)
        up = lax.rem(lax.div(there, 2) - plane + planes, planes)
        mark = 2 * up + jnp.where(lax.rem(there, 2) == core, 0, 1)
        mark = jnp.where(owner < 0, -1, mark)
        row = planes + away
        marks_ref[row : row + 1, :] = jnp.full((1, marks_ref.shape[1]), mark, jnp.int32)
    copy.wait()
    for away in range(planes):
        for other in range(2):
            outs[away][other] = held[table_ref[0, group_at(away, other, planes)]]


def plan(owner, grads):
    count, rows, cols = grads.shape
    planes = count // 2
    return pl.pallas_call(
        plan_kernel,
        out_shape=(
            shape_of(4, count + 1, dtype=jnp.int32),
            shape_of(2 * planes, 128, dtype=jnp.int32),
        )
        + (shape_of(2, rows, cols),) * planes,
        in_specs=[SMEM, ANY],
        out_specs=(SMEM,) + (VMEM,) * (planes + 1),
        scratch_shapes=[
            pltpu.SMEM((count + 1,), jnp.int32),
            pltpu.VMEM(grads.shape, grads.dtype),
            pltpu.SemaphoreType.DMA,
        ],
        compiler_params=params(8),
        name="plan",
    )(owner, grads)


def sort_kernel(*refs):
    ins, (own_ref, give_ref) = in_place(refs[:-2]), refs[-2:]
    for k, ref in enumerate(ins):
        own_ref[k] = ref[0]
        give_ref[k] = ref[1]


def sort(blocks):
    planes = len(blocks)
    _, rows, cols = blocks[0].shape
    return pl.pallas_call(
        sort_kernel,
        out_shape=(shape_of(planes, rows, cols),) * 2,
        in_specs=[VMEM] * planes,
        out_specs=(VMEM,) * 2,
        compiler_params=params(8),
        name="sort",
    )(*in_turn(blocks))


def split(number, shape):
    rest = jnp.broadcast_to(number, shape)
    row = lax.broadcasted_iota(jnp.int32, shape, 0)
    parts = jnp.zeros(shape, jnp.float32)
    for k in range(3):
        top = lax.reduce_precision(rest, 8, 7)
        parts = jnp.where(row == k, top, parts)
        rest = rest - top
    return parts.astype(jnp.bfloat16)


def gram_sums(own, got, acc, picked, write):
    each = own[0].shape[0] // BLOCK
    side = 2 * each
    turn = place_here()[0] * PIECE
    lists = (own, got)

    def block(s, i):
        start = (i % each) * BLOCK
        return lists[i // each][s][start : start + BLOCK, :]

    for s in range(len(own)):
        for i in range(side):
            start = pl.multiple_of((i % each) * BLOCK + turn, PIECE)
            picked[s, i * PIECE : (i + 1) * PIECE, :] = lists[i // each][s][pl.ds(start, PIECE), :]
    index = {pair: t for t, pair in enumerate(pairs_of(side * BLOCK))}
    for j in range(side):
        total = jnp.zeros(((side - j) * PIECE, BLOCK), jnp.float32)
        for s in range(len(own)):
            total = total + lax.dot_general(
                picked[s, j * PIECE :, :],
                block(s, j),
                (((1,), (1,)), ((), ())),
                preferred_element_type=jnp.float32,
            )
        for i in range(j, side):
            t = index[i, j]
            value = total[(i - j) * PIECE : (i - j + 1) * PIECE, :]
            write(t, value if acc is None else value + acc[t])
    total = jnp.zeros((1, BLOCK), jnp.float32)
    for s in range(len(own)):
        for i in range(side):
            values = block(s, i).astype(jnp.float32)
            total = total + jnp.sum(values * values, axis=0, keepdims=True)
    return jnp.sum(total, axis=1, keepdims=True)


def gram_first_kernel(*refs):
    own, got, (acc, square, picked) = refs[:6:2], (refs[1], refs[5], refs[3]), refs[6:]

    def write(t, value):
        acc[t] = value

    total = gram_sums(own, got, None, picked, write)
    square[...] = jnp.broadcast_to(total, square.shape)


def gram_last_kernel(own, got, acc, square, first, second, picked):
    cut = first.shape[0]

    def write(t, value):
        (first, second)[t // cut][t % cut] = value.astype(jnp.bfloat16)

    total = gram_sums([own], [got], acc, picked, write)
    second[second.shape[0] - 1] = split(total + square[0:1, :], (PIECE, BLOCK))


def gram_quarter(lists):
    own, got = lists
    rows = 2 * own[0].shape[0]
    blocks = len(pairs_of(rows))
    cut = (blocks + 1) // 2
    acc, square = pl.pallas_call(
        gram_first_kernel,
        out_shape=(
            shape_of(blocks, PIECE, BLOCK, dtype=jnp.float32),
            shape_of(8, BLOCK, dtype=jnp.float32),
        ),
        in_specs=[VMEM] * 6,
        out_specs=(VMEM,) * 2,
        scratch_shapes=[pltpu.VMEM((SIDE - 1, rows // SIDE, BLOCK), jnp.bfloat16)],
        compiler_params=params(16),
        cost_estimate=cost(3 * blocks * BLOCK**3 // 2, 4 * MIB),
        name="gram_first",
    )(own[0], got[0], own[1], got[3], own[3], got[1])
    return pl.pallas_call(
        gram_last_kernel,
        out_shape=(shape_of(cut, PIECE, BLOCK), shape_of(blocks + 1 - cut, PIECE, BLOCK)),
        in_specs=[VMEM] * 4,
        out_specs=(VMEM,) * 2,
        scratch_shapes=[pltpu.VMEM((1, rows // SIDE, BLOCK), jnp.bfloat16)],
        compiler_params=params(16),
        name="gram_last",
    )(own[2], got[2], acc, square)


def add_kernel(rows, *refs):
    lists, (first, second, inverse_ref) = in_lists(refs[: 2 * SIDE]), refs[2 * SIDE :]
    number = jnp.zeros((1, BLOCK), jnp.float32)
    for piece in lists[1]:
        last = piece.shape[0] - 1
        number = number + jnp.sum(piece[last].astype(jnp.float32), axis=0, keepdims=True)
    inverse = 1.0 / jnp.sqrt(number / rows + 1e-06)
    scale = inverse * inverse
    inverse_ref[...] = jnp.broadcast_to(inverse, inverse_ref.shape)
    for ins, out in zip(lists, (first, second)):
        total = ins[0][...].astype(jnp.float32)
        for other in ins[1:]:
            total = total + other[...].astype(jnp.float32)
        out[...] = jnp.where(scale > 0, total * scale, 0.0).astype(jnp.bfloat16)


def add(lists, rows):
    return pl.pallas_call(
        functools.partial(add_kernel, rows),
        out_shape=(
            shape_of(*lists[0][0].shape),
            shape_of(*lists[1][0].shape),
            shape_of(8, BLOCK, dtype=jnp.float32),
        ),
        in_specs=[VMEM] * (2 * SIDE),
        out_specs=(VMEM,) * 3,
        compiler_params=params(12),
        name="add",
    )(*out_of_lists(lists))


def step_kernel(pairs, factor, planes, own_ref, got_ref, inverse_ref, *refs):
    early, late = in_lists(refs[: 2 * SIDE])
    outs, (gram, normed, left) = refs[2 * SIDE : -3], refs[-3:]
    half = own_ref.shape[0]
    blocks = early[0].shape[0]
    side = 2 * half // BLOCK
    first, _ = place_here()
    for k, ref in enumerate((own_ref, got_ref)):
        for i in range(half // BLOCK):
            values = ref[i * BLOCK : (i + 1) * BLOCK, :].astype(jnp.float32)
            normed[k * half + i * BLOCK : k * half + (i + 1) * BLOCK, :] = (
                values * inverse_ref[0:1, :]
            ).astype(jnp.bfloat16)
    for t, (i, j) in enumerate(pairs):
        source, u = (early, t) if t < blocks else (late, t - blocks)
        for s in range(SIDE):
            p = lax.rem(first - s + SIDE, SIDE)
            rows = pl.ds(pl.multiple_of(i * BLOCK + p * PIECE, PIECE), PIECE)
            gram[rows, j * BLOCK : (j + 1) * BLOCK] = source[s][u]
    for i, j in pairs:
        if i != j:
            block = gram[i * BLOCK : (i + 1) * BLOCK, j * BLOCK : (j + 1) * BLOCK]
            gram[j * BLOCK : (j + 1) * BLOCK, i * BLOCK : (i + 1) * BLOCK] = block.T
    for i in range(side):
        rows = slice(i * BLOCK, (i + 1) * BLOCK)
        left[rows, :] = jnp.dot(
            gram[rows, :], normed[...], preferred_element_type=jnp.float32
        ).astype(jnp.bfloat16)
    each = half // planes
    for k in range(2):
        for away in range(0, planes, 2):
            rows = slice(k * half + away * each, k * half + (away + 2) * each)
            right = jnp.dot(gram[rows, :], left[...], preferred_element_type=jnp.float32)
            mixed = (
                3.4445 * normed[rows, :].astype(jnp.float32)
                - 4.775 * left[rows, :].astype(jnp.float32)
                + 2.0315 * right
            )
            values = (factor * mixed).astype(jnp.bfloat16)
            outs[away][k] = values[:each]
            outs[away + 1][k] = values[each:]


def step(own, got, inverse, lists, factor, planes):
    half, cols = own.shape
    rows = 2 * half
    return pl.pallas_call(
        functools.partial(step_kernel, pairs_of(rows), factor, planes),
        out_shape=(shape_of(2, half // planes, cols),) * planes,
        in_specs=[VMEM] * (3 + 2 * SIDE),
        out_specs=(VMEM,) * planes,
        scratch_shapes=[
            pltpu.VMEM((rows, rows), jnp.bfloat16),
            pltpu.VMEM((rows, cols), jnp.bfloat16),
            pltpu.VMEM((rows, cols), jnp.bfloat16),
        ],
        compiler_params=params(28),
        cost_estimate=cost(4 * rows * rows * cols, 6 * 1024 * 1024),
        name="step",
    )(own, got, inverse, *out_of_lists(lists))


def pick_kernel(planes, marks_ref, *refs):
    ins, (mine_ref, give_ref) = in_place(refs[:planes]), refs[planes:]
    for up, ref in enumerate(ins):
        mark = marks_ref[planes + up, 0]
        away = lax.div(jnp.maximum(mark, 0), 2)
        other = lax.rem(jnp.maximum(mark, 0), 2)

        @pl.when(jnp.logical_and(mark >= 0, other == 0))
        def _():
            mine_ref[away] = ref[...]

        @pl.when(jnp.logical_and(mark >= 0, other == 1))
        def _():
            give_ref[away] = ref[...]


def pick(marks, back):
    planes = len(back)
    block = back[0].shape
    return pl.pallas_call(
        functools.partial(pick_kernel, planes),
        out_shape=(shape_of(planes, *block),) * 2,
        in_specs=[VMEM] * (planes + 1),
        out_specs=(VMEM,) * 2,
        compiler_params=params(8),
        name="pick",
    )(marks, *in_turn(back))


def merge_kernel(marks_ref, mine_ref, got_ref, *outs):
    for away, out in enumerate(outs):
        mark = marks_ref[away, 0]

        @pl.when(mark < 0)
        def _():
            out[...] = jnp.zeros(out.shape, out.dtype)

        @pl.when(mark == 0)
        def _():
            out[...] = mine_ref[away]

        @pl.when(mark > 0)
        def _():
            out[0] = got_ref[away, 1]
            out[1] = got_ref[away, 0]


def merge(marks, mine, got):
    planes = mine.shape[0]
    return pl.pallas_call(
        merge_kernel,
        out_shape=(shape_of(*mine.shape[1:]),) * planes,
        in_specs=[VMEM] * 3,
        out_specs=(VMEM,) * planes,
        compiler_params=params(8),
        name="merge",
    )(marks, mine, got)


def update_kernel(planes, table_ref, *refs):
    own_ref, rest_ref, out_ref, sems = refs
    moves = []
    for away in range(planes):
        e = table_ref[0, group_at(away, 0, planes)]
        moves.append((own_ref.at[away], out_ref.at[e]))
        e = table_ref[0, group_at(away, 1, planes)]
        moves.append((rest_ref.at[away], out_ref.at[e]))
    move_all(moves, sems)


def update_of(table, own, rest):
    planes, rows, cols = rest.shape
    return pl.pallas_call(
        functools.partial(update_kernel, planes),
        out_shape=shape_of(2 * planes, rows, cols),
        in_specs=[SMEM] + [VMEM] * 2,
        out_specs=ANY,
        scratch_shapes=[pltpu.SemaphoreType.DMA((2 * planes,))],
        compiler_params=params(8),
        name="update",
    )(table, own, rest)


def slot_moves(ins, out_ref, slot):
    planes = len(ins)
    moves = []
    for away, ref in enumerate(ins):
        for k in range(2):
            rows = ref.shape[1]
            start = group_at(planes - away, k, planes) * rows
            to = out_ref.at[slot, pl.ds(pl.multiple_of(start, rows), rows)]
            moves.append((ref.at[k], to))
    return moves


def first_kernel(planes, table_ref, *refs):
    ins, (out_ref, zero, sems) = refs[:planes], refs[planes:]
    moves = slot_moves(ins, out_ref, 0)
    owns = table_ref[1, group_at(0, 0, planes)] > 0

    @pl.when(owns)
    def _():
        move_all(moves, sems)

    @pl.when(jnp.logical_not(owns))
    def _():
        zero[...] = jnp.zeros(zero.shape, zero.dtype)
        move_all([(zero, b) for _, b in moves], sems)


def second_kernel(planes, *refs):
    ins, (_, out_ref, sems) = in_place(refs[:planes]), refs[planes:]
    move_all(slot_moves(ins, out_ref, 1), sems)


def first_slot(table, done):
    planes = len(done)
    _, rows, cols = done[0].shape
    return pl.pallas_call(
        functools.partial(first_kernel, planes),
        out_shape=shape_of(MOST, 2 * planes * rows, cols),
        in_specs=[SMEM] + [VMEM] * planes,
        out_specs=ANY,
        scratch_shapes=[
            pltpu.VMEM((rows, cols), jnp.bfloat16),
            pltpu.SemaphoreType.DMA((2 * planes,)),
        ],
        compiler_params=params(8),
        name="first_slot",
    )(table, *done)


def second_slot(came, owned):
    planes = len(came)
    return pl.pallas_call(
        functools.partial(second_kernel, planes),
        out_shape=shape_of(*owned.shape),
        in_specs=[VMEM] * planes + [ANY],
        out_specs=ANY,
        scratch_shapes=[pltpu.SemaphoreType.DMA((2 * planes,))],
        input_output_aliases={planes: 0},
        compiler_params=params(8),
        name="second_slot",
    )(*in_turn(came), owned)


def neighbour(value, order, amount):
    groups, places = lax.axis_size("fsdp"), SIDE * SIDE
    moves = []
    for at in range(groups * places):
        group, place = divmod(at, places)
        y, x = divmod(place, SIDE)
        if group % 2 == order:
            x = (x + amount) % SIDE
        else:
            y = (y + amount) % SIDE
        moves.append((at, group * places + y * SIDE + x))
    return lax.ppermute(value, ("fsdp", "grp"), moves)


def gather(first, second, order):
    one = [first, neighbour(first, order, 1), None, neighbour(first, order, -1)]
    two = [second, neighbour(second, order, 1), None, neighbour(second, order, -1)]
    one[2] = neighbour(one[1], order, 1)
    two[2] = neighbour(two[3], order, -1)
    return one, two


TRAVEL = ((0, 0), (1, 0), (0, 1), (1, 3), (0, 3), (1, 1), (0, 2), (1, 2))


def out_of_lists(lists):
    return [lists[k][s] for k, s in TRAVEL]


def in_lists(refs):
    return [[refs[TRAVEL.index((k, s))] for s in range(SIDE)] for k in range(2)]


def over_planes(blocks, sign):
    planes = len(blocks)
    got = list(blocks)
    for away in farthest_first(planes)[1:]:
        moves = []
        for group in range(2 * planes):
            plane, core = divmod(group, 2)
            moves.append((group, 2 * ((plane + sign * away) % planes) + core))
        got[away] = lax.ppermute(blocks[away], "fsdp", moves)
    return got


def farthest_first(planes):
    return sorted(range(planes), key=lambda a: -min(a, planes - a) if a else -planes)


def in_turn(blocks):
    return [blocks[away] for away in farthest_first(len(blocks))]


def in_place(refs):
    order = farthest_first(len(refs))
    return [refs[order.index(away)] for away in range(len(refs))]


def swap(value):
    groups = lax.axis_size("fsdp")
    return lax.ppermute(value, "fsdp", [(g, g ^ 1) for g in range(groups)])


def on_device(grads, owner):
    count, rows_dev, cols_dev = grads.shape
    groups = lax.axis_size("fsdp")
    planes = groups // 2
    rows = rows_dev * groups
    cols = cols_dev * lax.axis_size("grp")
    factor = 0.2 * math.sqrt(max(rows, cols))
    table, marks, *sends = plan(owner, grads)
    own, give = sort(over_planes(sends, 1))
    got = swap(give)
    own, got = own.reshape(rows // 2, cols_dev), got.reshape(rows // 2, cols_dev)
    parts = gram_quarter(gather(own, got, 0))
    *parts, inverse = add(gather(*parts, 1), rows)
    done = step(own, got, inverse, gather(*parts, 0), factor, planes)
    back = over_planes(done, -1)
    mine, give = pick(marks, back)
    sends = merge(marks, mine, swap(give))
    came = over_planes(sends, 1)
    own, rest = sort(back)
    update = update_of(table, own, swap(rest))
    owned = second_slot(came, first_slot(table, done))
    return (update, owned)


def solution(mesh):
    return jax.shard_map(
        on_device,
        mesh=mesh,
        in_specs=(P(None, "fsdp", "grp"), P()),
        out_specs=(P(None, "fsdp", "grp"), P("fsdp", None, "grp")),
        check_vma=False,
    )
```

```python
import functools
import math

import jax
import jax.numpy as jnp
from jax import lax
from jax.experimental import pallas as pl
from jax.experimental.pallas import tpu as pltpu
from jax.sharding import PartitionSpec as P

MOST = 2
SIDE = 4
BLOCK = 256
PIECE = BLOCK // SIDE
MIB = 1024 * 1024

VMEM = pl.BlockSpec(memory_space=pltpu.VMEM)
SMEM = pl.BlockSpec(memory_space=pltpu.SMEM)
ANY = pl.BlockSpec(memory_space=pl.ANY)


def params(mib):
    return pltpu.CompilerParams(vmem_limit_bytes=mib * MIB)


def shape_of(*dims, dtype=jnp.bfloat16):
    return jax.ShapeDtypeStruct(dims, dtype)


def cost(flops, size):
    return pl.CostEstimate(flops=flops, bytes_accessed=size, transcendentals=0)


def spot_here():
    me = lax.axis_index("fsdp")
    return lax.div(me, 2), lax.rem(me, 2)


def place_here():
    at = lax.axis_index("grp")
    x, y = lax.rem(at, SIDE), lax.div(at, SIDE)
    _, core = spot_here()
    return jnp.where(core == 0, x, y), jnp.where(core == 0, y, x)


def pairs_of(rows):
    side = rows // BLOCK
    return [(i, j) for i in range(side) for j in range(i + 1)]


def move_all(moves, sems):
    copies = [pltpu.make_async_copy(a, b, sems.at[k]) for k, (a, b) in enumerate(moves)]
    for copy in copies:
        copy.start()
    for copy in copies:
        copy.wait()


def group_at(away, other, planes):
    plane, core = spot_here()
    return 2 * lax.rem(plane + away, planes) + (1 - core if other else core)


def plan_kernel(owner_ref, grads_ref, table_ref, marks_ref, *refs):
    outs, (empty_ref, held, sem) = refs[:-3], refs[-3:]
    count, planes = owner_ref.shape[0], len(outs)
    copy = pltpu.make_async_copy(grads_ref, held, sem)
    copy.start()
    for g in range(count):
        table_ref[1, g] = 0
        table_ref[2, g] = -1
        table_ref[3, g] = -1
    for e in range(count):
        g = owner_ref[e]
        seen = table_ref[1, g]
        table_ref[1, g] = seen + 1
        table_ref[jnp.where(seen == 0, 0, 2), g] = e
    n = jnp.int32(0)
    for g in range(count):
        empty_ref[n] = g
        n = n + (table_ref[1, g] == 0).astype(jnp.int32)
    n = jnp.int32(0)
    for g in range(count):
        e = table_ref[2, g]
        two = e >= 0
        h = jnp.where(two, empty_ref[n], count)
        table_ref[2, g] = jnp.where(two, h, -1)
        table_ref[0, h] = e
        table_ref[3, h] = g
        n = n + two.astype(jnp.int32)
    plane, core = spot_here()
    for away in range(planes):
        group = group_at(away, 0, planes)
        helper = table_ref[2, group]
        here = jnp.where(lax.rem(jnp.maximum(helper, 0), 2) == core, 0, 1)
        mark = jnp.where(helper < 0, -1, here)
        marks_ref[away : away + 1, :] = jnp.full((1, marks_ref.shape[1]), mark, jnp.int32)
        owner = table_ref[3, group]
        there = jnp.maximum(owner, 0)
        up = lax.rem(lax.div(there, 2) - plane + planes, planes)
        mark = 2 * up + jnp.where(lax.rem(there, 2) == core, 0, 1)
        mark = jnp.where(owner < 0, -1, mark)
        row = planes + away
        marks_ref[row : row + 1, :] = jnp.full((1, marks_ref.shape[1]), mark, jnp.int32)
    copy.wait()
    for away in range(planes):
        for other in range(2):
            outs[away][other] = held[table_ref[0, group_at(away, other, planes)]]


def plan(owner, grads):
    count, rows, cols = grads.shape
    planes = count // 2
    return pl.pallas_call(
        plan_kernel,
        out_shape=(
            shape_of(4, count + 1, dtype=jnp.int32),
            shape_of(2 * planes, 128, dtype=jnp.int32),
        )
        + (shape_of(2, rows, cols),) * planes,
        in_specs=[SMEM, ANY],
        out_specs=(SMEM,) + (VMEM,) * (planes + 1),
        scratch_shapes=[
            pltpu.SMEM((count + 1,), jnp.int32),
            pltpu.VMEM(grads.shape, grads.dtype),
            pltpu.SemaphoreType.DMA,
        ],
        compiler_params=params(8),
        name="plan",
    )(owner, grads)


def sort_kernel(*refs):
    ins, (own_ref, give_ref) = in_place(refs[:-2]), refs[-2:]
    for k, ref in enumerate(ins):
        own_ref[k] = ref[0]
        give_ref[k] = ref[1]


def sort(blocks):
    planes = len(blocks)
    _, rows, cols = blocks[0].shape
    return pl.pallas_call(
        sort_kernel,
        out_shape=(shape_of(planes, rows, cols),) * 2,
        in_specs=[VMEM] * planes,
        out_specs=(VMEM,) * 2,
        compiler_params=params(8),
        name="sort",
    )(*in_turn(blocks))


def split(number, shape):
    rest = jnp.broadcast_to(number, shape)
    row = lax.broadcasted_iota(jnp.int32, shape, 0)
    parts = jnp.zeros(shape, jnp.float32)
    for k in range(3):
        top = lax.reduce_precision(rest, 8, 7)
        parts = jnp.where(row == k, top, parts)
        rest = rest - top
    return parts.astype(jnp.bfloat16)


def gram_sums(own, got, acc, picked, write):
    each = own[0].shape[0] // BLOCK
    side = 2 * each
    turn = place_here()[0] * PIECE
    lists = (own, got)

    def block(s, i):
        start = (i % each) * BLOCK
        return lists[i // each][s][start : start + BLOCK, :]

    for s in range(len(own)):
        for i in range(side):
            start = pl.multiple_of((i % each) * BLOCK + turn, PIECE)
            picked[s, i * PIECE : (i + 1) * PIECE, :] = lists[i // each][s][pl.ds(start, PIECE), :]
    index = {pair: t for t, pair in enumerate(pairs_of(side * BLOCK))}
    for j in range(side):
        total = jnp.zeros(((side - j) * PIECE, BLOCK), jnp.float32)
        for s in range(len(own)):
            total = total + lax.dot_general(
                picked[s, j * PIECE :, :],
                block(s, j),
                (((1,), (1,)), ((), ())),
                preferred_element_type=jnp.float32,
            )
        for i in range(j, side):
            t = index[i, j]
            value = total[(i - j) * PIECE : (i - j + 1) * PIECE, :]
            write(t, value if acc is None else value + acc[t])
    total = jnp.zeros((1, BLOCK), jnp.float32)
    for s in range(len(own)):
        for i in range(side):
            values = block(s, i).astype(jnp.float32)
            total = total + jnp.sum(values * values, axis=0, keepdims=True)
    return jnp.sum(total, axis=1, keepdims=True)


def gram_first_kernel(*refs):
    own, got, (acc, square, picked) = refs[:6:2], (refs[1], refs[5], refs[3]), refs[6:]

    def write(t, value):
        acc[t] = value

    total = gram_sums(own, got, None, picked, write)
    square[...] = jnp.broadcast_to(total, square.shape)


def gram_last_kernel(own, got, acc, square, first, second, picked):
    cut = first.shape[0]

    def write(t, value):
        (first, second)[t // cut][t % cut] = value.astype(jnp.bfloat16)

    total = gram_sums([own], [got], acc, picked, write)
    second[second.shape[0] - 1] = split(total + square[0:1, :], (PIECE, BLOCK))


def gram_quarter(lists):
    own, got = lists
    rows = 2 * own[0].shape[0]
    blocks = len(pairs_of(rows))
    cut = (blocks + 1) // 2
    acc, square = pl.pallas_call(
        gram_first_kernel,
        out_shape=(
            shape_of(blocks, PIECE, BLOCK, dtype=jnp.float32),
            shape_of(8, BLOCK, dtype=jnp.float32),
        ),
        in_specs=[VMEM] * 6,
        out_specs=(VMEM,) * 2,
        scratch_shapes=[pltpu.VMEM((SIDE - 1, rows // SIDE, BLOCK), jnp.bfloat16)],
        compiler_params=params(16),
        cost_estimate=cost(3 * blocks * BLOCK**3 // 2, 4 * MIB),
        name="gram_first",
    )(own[0], got[0], own[1], got[3], own[3], got[1])
    return pl.pallas_call(
        gram_last_kernel,
        out_shape=(shape_of(cut, PIECE, BLOCK), shape_of(blocks + 1 - cut, PIECE, BLOCK)),
        in_specs=[VMEM] * 4,
        out_specs=(VMEM,) * 2,
        scratch_shapes=[pltpu.VMEM((1, rows // SIDE, BLOCK), jnp.bfloat16)],
        compiler_params=params(16),
        name="gram_last",
    )(own[2], got[2], acc, square)


def add_kernel(rows, *refs):
    lists, (first, second, inverse_ref) = in_lists(refs[: 2 * SIDE]), refs[2 * SIDE :]
    number = jnp.zeros((1, BLOCK), jnp.float32)
    for piece in lists[1]:
        last = piece.shape[0] - 1
        number = number + jnp.sum(piece[last].astype(jnp.float32), axis=0, keepdims=True)
    inverse = 1.0 / jnp.sqrt(number / rows + 1e-06)
    scale = inverse * inverse
    inverse_ref[...] = jnp.broadcast_to(inverse, inverse_ref.shape)
    for ins, out in zip(lists, (first, second)):
        total = ins[0][...].astype(jnp.float32)
        for other in ins[1:]:
            total = total + other[...].astype(jnp.float32)
        out[...] = jnp.where(scale > 0, total * scale, 0.0).astype(jnp.bfloat16)


def add(lists, rows):
    return pl.pallas_call(
        functools.partial(add_kernel, rows),
        out_shape=(
            shape_of(*lists[0][0].shape),
            shape_of(*lists[1][0].shape),
            shape_of(8, BLOCK, dtype=jnp.float32),
        ),
        in_specs=[VMEM] * (2 * SIDE),
        out_specs=(VMEM,) * 3,
        compiler_params=params(12),
        name="add",
    )(*out_of_lists(lists))


def step_kernel(pairs, factor, planes, own_ref, got_ref, inverse_ref, *refs):
    early, late = in_lists(refs[: 2 * SIDE])
    outs, (gram, normed, left) = refs[2 * SIDE : -3], refs[-3:]
    half = own_ref.shape[0]
    blocks = early[0].shape[0]
    side = 2 * half // BLOCK
    first, _ = place_here()
    for k, ref in enumerate((own_ref, got_ref)):
        for i in range(half // BLOCK):
            values = ref[i * BLOCK : (i + 1) * BLOCK, :].astype(jnp.float32)
            normed[k * half + i * BLOCK : k * half + (i + 1) * BLOCK, :] = (
                values * inverse_ref[0:1, :]
            ).astype(jnp.bfloat16)
    for t, (i, j) in enumerate(pairs):
        source, u = (early, t) if t < blocks else (late, t - blocks)
        for s in range(SIDE):
            p = lax.rem(first - s + SIDE, SIDE)
            rows = pl.ds(pl.multiple_of(i * BLOCK + p * PIECE, PIECE), PIECE)
            gram[rows, j * BLOCK : (j + 1) * BLOCK] = source[s][u]
    for i, j in pairs:
        if i != j:
            block = gram[i * BLOCK : (i + 1) * BLOCK, j * BLOCK : (j + 1) * BLOCK]
            gram[j * BLOCK : (j + 1) * BLOCK, i * BLOCK : (i + 1) * BLOCK] = block.T
    for i in range(side):
        rows = slice(i * BLOCK, (i + 1) * BLOCK)
        left[rows, :] = jnp.dot(
            gram[rows, :], normed[...], preferred_element_type=jnp.float32
        ).astype(jnp.bfloat16)
    each = half // planes
    for k in range(2):
        for away in range(0, planes, 2):
            rows = slice(k * half + away * each, k * half + (away + 2) * each)
            right = jnp.dot(gram[rows, :], left[...], preferred_element_type=jnp.float32)
            mixed = (
                3.4445 * normed[rows, :].astype(jnp.float32)
                - 4.775 * left[rows, :].astype(jnp.float32)
                + 2.0315 * right
            )
            values = (factor * mixed).astype(jnp.bfloat16)
            outs[away][k] = values[:each]
            outs[away + 1][k] = values[each:]


def step(own, got, inverse, lists, factor, planes):
    half, cols = own.shape
    rows = 2 * half
    return pl.pallas_call(
        functools.partial(step_kernel, pairs_of(rows), factor, planes),
        out_shape=(shape_of(2, half // planes, cols),) * planes,
        in_specs=[VMEM] * (3 + 2 * SIDE),
        out_specs=(VMEM,) * planes,
        scratch_shapes=[
            pltpu.VMEM((rows, rows), jnp.bfloat16),
            pltpu.VMEM((rows, cols), jnp.bfloat16),
            pltpu.VMEM((rows, cols), jnp.bfloat16),
        ],
        compiler_params=params(28),
        cost_estimate=cost(4 * rows * rows * cols, 6 * 1024 * 1024),
        name="step",
    )(own, got, inverse, *out_of_lists(lists))


def pick_kernel(planes, marks_ref, *refs):
    ins, (mine_ref, give_ref) = in_place(refs[:planes]), refs[planes:]
    for up, ref in enumerate(ins):
        mark = marks_ref[planes + up, 0]
        away = lax.div(jnp.maximum(mark, 0), 2)
        other = lax.rem(jnp.maximum(mark, 0), 2)

        @pl.when(jnp.logical_and(mark >= 0, other == 0))
        def _():
            mine_ref[away] = ref[...]

        @pl.when(jnp.logical_and(mark >= 0, other == 1))
        def _():
            give_ref[away] = ref[...]


def pick(marks, back):
    planes = len(back)
    block = back[0].shape
    return pl.pallas_call(
        functools.partial(pick_kernel, planes),
        out_shape=(shape_of(planes, *block),) * 2,
        in_specs=[VMEM] * (planes + 1),
        out_specs=(VMEM,) * 2,
        compiler_params=params(8),
        name="pick",
    )(marks, *in_turn(back))


def merge_kernel(marks_ref, mine_ref, got_ref, *outs):
    for away, out in enumerate(outs):
        mark = marks_ref[away, 0]

        @pl.when(mark < 0)
        def _():
            out[...] = jnp.zeros(out.shape, out.dtype)

        @pl.when(mark == 0)
        def _():
            out[...] = mine_ref[away]

        @pl.when(mark > 0)
        def _():
            out[0] = got_ref[away, 1]
            out[1] = got_ref[away, 0]


def merge(marks, mine, got):
    planes = mine.shape[0]
    return pl.pallas_call(
        merge_kernel,
        out_shape=(shape_of(*mine.shape[1:]),) * planes,
        in_specs=[VMEM] * 3,
        out_specs=(VMEM,) * planes,
        compiler_params=params(8),
        name="merge",
    )(marks, mine, got)


def update_kernel(planes, table_ref, *refs):
    own_ref, rest_ref, out_ref, sems = refs
    moves = []
    for away in range(planes):
        e = table_ref[0, group_at(away, 0, planes)]
        moves.append((own_ref.at[away], out_ref.at[e]))
        e = table_ref[0, group_at(away, 1, planes)]
        moves.append((rest_ref.at[away], out_ref.at[e]))
    move_all(moves, sems)


def update_of(table, own, rest):
    planes, rows, cols = rest.shape
    return pl.pallas_call(
        functools.partial(update_kernel, planes),
        out_shape=shape_of(2 * planes, rows, cols),
        in_specs=[SMEM] + [VMEM] * 2,
        out_specs=ANY,
        scratch_shapes=[pltpu.SemaphoreType.DMA((2 * planes,))],
        compiler_params=params(8),
        name="update",
    )(table, own, rest)


def slot_moves(ins, out_ref, slot):
    planes = len(ins)
    moves = []
    for away, ref in enumerate(ins):
        for k in range(2):
            rows = ref.shape[1]
            start = group_at(planes - away, k, planes) * rows
            to = out_ref.at[slot, pl.ds(pl.multiple_of(start, rows), rows)]
            moves.append((ref.at[k], to))
    return moves


def first_kernel(planes, table_ref, *refs):
    ins, (out_ref, zero, sems) = refs[:planes], refs[planes:]
    moves = slot_moves(ins, out_ref, 0)
    owns = table_ref[1, group_at(0, 0, planes)] > 0

    @pl.when(owns)
    def _():
        move_all(moves, sems)

    @pl.when(jnp.logical_not(owns))
    def _():
        zero[...] = jnp.zeros(zero.shape, zero.dtype)
        move_all([(zero, b) for _, b in moves], sems)


def second_kernel(planes, *refs):
    ins, (_, out_ref, sems) = in_place(refs[:planes], 1), refs[planes:]
    move_all(slot_moves(ins, out_ref, 1), sems)


def first_slot(table, done):
    planes = len(done)
    _, rows, cols = done[0].shape
    return pl.pallas_call(
        functools.partial(first_kernel, planes),
        out_shape=shape_of(MOST, 2 * planes * rows, cols),
        in_specs=[SMEM] + [VMEM] * planes,
        out_specs=ANY,
        scratch_shapes=[
            pltpu.VMEM((rows, cols), jnp.bfloat16),
            pltpu.SemaphoreType.DMA((2 * planes,)),
        ],
        compiler_params=params(8),
        name="first_slot",
    )(table, *done)


def second_slot(came, owned):
    planes = len(came)
    return pl.pallas_call(
        functools.partial(second_kernel, planes),
        out_shape=shape_of(*owned.shape),
        in_specs=[VMEM] * planes + [ANY],
        out_specs=ANY,
        scratch_shapes=[pltpu.SemaphoreType.DMA((2 * planes,))],
        input_output_aliases={planes: 0},
        compiler_params=params(8),
        name="second_slot",
    )(*in_turn(came, 1), owned)


def neighbour(value, order, amount):
    groups, places = lax.axis_size("fsdp"), SIDE * SIDE
    moves = []
    for at in range(groups * places):
        group, place = divmod(at, places)
        y, x = divmod(place, SIDE)
        if group % 2 == order:
            x = (x + amount) % SIDE
        else:
            y = (y + amount) % SIDE
        moves.append((at, group * places + y * SIDE + x))
    return lax.ppermute(value, ("fsdp", "grp"), moves)


def gather(first, second, order):
    one = [first, neighbour(first, order, 1), None, neighbour(first, order, -1)]
    two = [second, neighbour(second, order, 1), None, neighbour(second, order, -1)]
    one[2] = neighbour(one[1], order, 1)
    two[2] = neighbour(two[3], order, -1)
    return one, two


TRAVEL = ((0, 0), (1, 0), (0, 1), (1, 3), (0, 3), (1, 1), (0, 2), (1, 2))


def out_of_lists(lists):
    return [lists[k][s] for k, s in TRAVEL]


def in_lists(refs):
    return [[refs[TRAVEL.index((k, s))] for s in range(SIDE)] for k in range(2)]


def over_planes(blocks, sign):
    planes = len(blocks)
    got = list(blocks)
    for away in range(1, planes):
        moves = []
        for group in range(2 * planes):
            plane, core = divmod(group, 2)
            moves.append((group, 2 * ((plane + sign * away) % planes) + core))
        got[away] = lax.ppermute(blocks[away], "fsdp", moves)
    return got


def by_distance(planes, sign=-1):
    return [0] + sorted(range(1, planes), key=lambda a: sign * min(a, planes - a))


def in_turn(blocks, sign=-1):
    return [blocks[away] for away in by_distance(len(blocks), sign)]


def in_place(refs, sign=-1):
    order = by_distance(len(refs), sign)
    return [refs[order.index(away)] for away in range(len(refs))]


def swap(value):
    groups = lax.axis_size("fsdp")
    return lax.ppermute(value, "fsdp", [(g, g ^ 1) for g in range(groups)])


def on_device(grads, owner):
    count, rows_dev, cols_dev = grads.shape
    groups = lax.axis_size("fsdp")
    planes = groups // 2
    rows = rows_dev * groups
    cols = cols_dev * lax.axis_size("grp")
    factor = 0.2 * math.sqrt(max(rows, cols))
    table, marks, *sends = plan(owner, grads)
    own, give = sort(over_planes(sends, 1))
    got = swap(give)
    own, got = own.reshape(rows // 2, cols_dev), got.reshape(rows // 2, cols_dev)
    parts = gram_quarter(gather(own, got, 0))
    *parts, inverse = add(gather(*parts, 1), rows)
    done = step(own, got, inverse, gather(*parts, 0), factor, planes)
    back = over_planes(done, -1)
    mine, give = pick(marks, back)
    sends = merge(marks, mine, swap(give))
    came = over_planes(sends, 1)
    own, rest = sort(back)
    update = update_of(table, own, swap(rest))
    owned = second_slot(came, first_slot(table, done))
    return (update, owned)


def solution(mesh):
    return jax.shard_map(
        on_device,
        mesh=mesh,
        in_specs=(P(None, "fsdp", "grp"), P()),
        out_specs=(P(None, "fsdp", "grp"), P("fsdp", None, "grp")),
        check_vma=False,
    )
```
